128 devices in a mesh: dp: 8 (over y, z_hi), mp: 16 (over z_lo, x, core).
Axes of the slice: x: 4, y: 4, z: 4 (z_hi: 2, z_lo: 2; z = z_hi * 2 + z_lo), core: 2. Of those that a mesh axis runs over, the one named last changes fastest.
Arguments:
- tokens: bfloat16 [3072, 6144], P(('dp', 'mp')), may hold values from -24 to 24
- out_cotangent: bfloat16 [3072, 6144], P(('dp', 'mp')), may hold values from -24 to 24
- weight_in: bfloat16 [6144, 12288], P(None, 'mp'), may hold values from -0.078125 to 0.078125
- weight_out: bfloat16 [12288, 6144], P('mp'), may hold values from -0.0546875 to 0.0546875
Outputs:
- block_output: bfloat16 [3072, 6144], P(('dp', 'mp'))
- token_grad: bfloat16 [3072, 6144], P(('dp', 'mp'))
- grad_in: bfloat16 [6144, 12288], P('dp', 'mp')
- grad_out: bfloat16 [12288, 6144], P('mp', 'dp')
The draws below stay inside these ranges and needn't reach their ends.
All inputs are finite; a program needn't handle non-finite values.
Results may differ from the reference program's by a relative error of at most 0.023.
Values may be sent and summed in bfloat16 or wider, within the bound.
A program may use at most 128 MiB of HBM per device.

```python
import jax
import jax.numpy as jnp
from jax import lax

D = 6144
FF = 12288
TOK_DEV = 24
TOKENS = 3072
N_DP = 8
N_MP = 16


def spiked(values, own_key, source, target, blocks, factor):
    def block_of(dim):
        return (jnp.arange(values.shape[dim]) // (values.shape[dim] // blocks)).reshape((-1,) + (1,) * (values.ndim - 1 - dim))

    one_side = jax.random.permutation(own_key, blocks)[block_of(target)]
    far = (block_of(target) + blocks // 2) % blocks
    return jnp.where((block_of(source) == one_side) | (block_of(source) == far), factor * values, values)


def steps_of(key, dims, shards, smallest, high):
    def one(axis_at, blocks):
        heights = jax.random.uniform(jax.random.fold_in(jax.random.fold_in(key, 6), axis_at), (blocks,), jnp.float32, smallest / len(shards), high / len(shards))
        return jnp.repeat(jnp.exp(heights), dims[axis_at] // blocks).reshape((-1,) + (1,) * (len(dims) - axis_at - 1))

    factor_of = one(*shards[0])
    for cut in shards[1:]:
        factor_of = factor_of * one(*cut)
    return factor_of


def centred(stream_key, dims, scale, reach, pieces=(), dtype=jnp.bfloat16):
    drawn = jax.random.normal(stream_key, dims, jnp.float32) * scale
    if len(pieces) > 0:
        drawn = steps_of(stream_key, dims, pieces, -0.22, 0.18) * drawn
    return jnp.clip(drawn, min=-reach, max=reach).astype(dtype)


def heavy_noise(stream_key, dims, deviation, bound, shards, heavy, dtype=jnp.bfloat16):
    result = deviation * jax.random.normal(stream_key, dims, jnp.float32)
    if shards:
        result = result * steps_of(stream_key, dims, shards, -0.22, 0.18)
    return jnp.clip(spiked(result, jax.random.fold_in(stream_key, 3), *heavy), -bound, bound).astype(dtype)


def setup_inputs(seed: int = 0) -> dict:
    arg_keys = jax.random.split(jax.random.key(seed), 5)
    return {
        "tokens": heavy_noise(arg_keys[0], (TOKENS, D), 1.0, 24.0, ((0, 128),), (0, 1, 128, 5.5)),
        "out_cotangent": heavy_noise(arg_keys[1], (TOKENS, D), 1.0, 24.0, ((0, 128),), (0, 1, 128, 5.5)),
        "weight_in": centred(arg_keys[2], (D, FF), D ** -0.5, 0.078125, ((1, 16),)),
        "weight_out": centred(arg_keys[3], (FF, D), FF ** -0.5, 0.0546875, ((0, 16),)),
    }


root_coeff = 0.7978845608028654
cubic_coeff = 0.044715


def gelu_value(u):
    inner = root_coeff * (u + cubic_coeff * u * u * u)
    return 0.5 * u * (1.0 + jnp.tanh(inner))


def gelu_slope(u):
    inner = root_coeff * (u + cubic_coeff * u * u * u)
    tanh_value = jnp.tanh(inner)
    return 0.5 * (1.0 + tanh_value) + 0.5 * u * (1.0 - tanh_value * tanh_value) * root_coeff * (1.0 + 3.0 * cubic_coeff * u * u)


def block_partials(left, right):
    rows = left.shape[0]
    lhs = left.astype(jnp.float32).reshape(rows, N_MP, -1)
    rhs = right.astype(jnp.float32).reshape(N_MP, -1, right.shape[1])
    parts = jnp.einsum("rkf,kfd->krd", lhs, rhs)
    rounded = lax.optimization_barrier(parts.astype(jnp.bfloat16))
    return jnp.sum(rounded.astype(jnp.float32), axis=0)


def reference(tokens, out_cotangent, weight_in, weight_out):
    group_rows = TOK_DEV * N_MP
    token_groups = tokens.reshape(N_DP, group_rows, D)
    cotangent_groups = out_cotangent.reshape(N_DP, group_rows, D)
    weight_in_t = weight_in.T
    weight_out_t = weight_out.T

    def one_group(carry, pair):
        sum_in, sum_out = carry
        rows_x, rows_g = pair
        preact = jnp.dot(rows_x, weight_in, preferred_element_type=jnp.float32)
        hidden = gelu_value(preact).astype(jnp.bfloat16)
        output = block_partials(hidden, weight_out).astype(jnp.bfloat16)
        hidden_grad = jnp.dot(rows_g, weight_out_t, preferred_element_type=jnp.float32)
        preact_grad = (hidden_grad * gelu_slope(preact)).astype(jnp.bfloat16)
        token_grad = block_partials(preact_grad, weight_in_t).astype(jnp.bfloat16)
        term_in = jnp.dot(rows_x.T, preact_grad, preferred_element_type=jnp.float32).astype(jnp.bfloat16)
        term_out = jnp.dot(hidden.T, rows_g, preferred_element_type=jnp.float32).astype(jnp.bfloat16)
        sum_in = sum_in + term_in.astype(jnp.float32)
        sum_out = sum_out + term_out.astype(jnp.float32)
        return (sum_in, sum_out), (output, token_grad)

    start = (jnp.zeros((D, FF), jnp.float32), jnp.zeros((FF, D), jnp.float32))
    (sum_in, sum_out), (outputs, grads) = lax.scan(one_group, start, (token_groups, cotangent_groups))
    factor = float(TOKENS) ** -0.5
    block_output = outputs.reshape(TOKENS, D)
    token_grad = grads.reshape(TOKENS, D)
    return block_output, token_grad, (sum_in * factor).astype(jnp.bfloat16), (sum_out * factor).astype(jnp.bfloat16)
```

```python
import functools

import jax
import jax.numpy as jnp
from jax import lax
from jax.experimental import pallas as pl
from jax.experimental.pallas import tpu as pltpu
from jax.sharding import PartitionSpec as P

MESH = pl.DeviceIdType.MESH
BF16 = jnp.bfloat16
F32 = jnp.float32
D = 6144
HALF = 3072
QUARTER = 1536
BLOCK = 768
ROWS = 384
UNIT = 48
PAIR = 96
FH = 768
CHUNK = 1024
N_COPIES = 132
FACTOR = 3072.0**-0.5

root_coeff = 0.7978845608028654
cubic_coeff = 0.044715


def mul(value, step):
    return pl.multiple_of(value * step, step)


def dot(left, right):
    return jnp.dot(left, right, preferred_element_type=F32)


def dot_nt(left, right):
    return lax.dot_general(left, right, (((1,), (1,)), ((), ())), preferred_element_type=F32)


def kernel(
    tx, tg, w1_hbm, w2_hbm,
    out_o, tok_o, gi_o, go_o,
    w1, w2, xb, gb, pb, xc, gc, ht, pt, sh, acc, acc2, hb, rcore, rx, rz, rf, zr,
    lsem, ssem, rsem, credit,
):
    dp, mp = lax.axis_index("dp"), lax.axis_index("mp")
    y, zh = lax.div(dp, 2), lax.rem(dp, 2)
    zl, x, c = lax.div(mp, 8), lax.rem(lax.div(mp, 2), 4), lax.rem(mp, 2)
    oc, ozl, ozh = 1 - c, 1 - zl, 1 - zh

    def ring(value, shift):
        return lax.rem(value + shift, 4)

    core_peer = (dp, zl * 8 + x * 2 + oc)
    zl_peer = (dp, ozl * 8 + x * 2 + c)
    zh_peer = (y * 2 + ozh, mp)

    def x_peer(shift):
        return (dp, zl * 8 + ring(x, shift) * 2 + c)

    def y_peer(shift):
        return (ring(y, shift) * 2 + zh, mp)

    counter = [0]
    sent, done = [], set()

    def copy(src, dst, device, landing=None):
        at = counter[0]
        counter[0] += 1
        started = pltpu.make_async_remote_copy(
            src_ref=src, dst_ref=dst, send_sem=ssem.at[at], recv_sem=rsem.at[at],
            device_id=device, device_id_type=MESH,
        )
        started.start()
        here = started
        if landing is not None:
            here = pltpu.make_async_remote_copy(
                src_ref=src, dst_ref=landing, send_sem=ssem.at[at], recv_sem=rsem.at[at],
                device_id=device, device_id_type=MESH,
            )
        sent.append(started)
        return here, started

    def finish_sends(pairs):
        for _, started in pairs:
            started.wait_send()
            done.add(id(started))

    barrier = pltpu.get_barrier_semaphore()
    peers = [core_peer, zl_peer, zh_peer] + [x_peer(s) for s in (1, 2, 3)] + [y_peer(s) for s in (1, 2, 3)]
    for peer in peers:
        pl.semaphore_signal(barrier, inc=1, device_id=peer, device_id_type=MESH)
    pl.semaphore_wait(barrier, len(peers))

    def local(src, dst, at):
        started = pltpu.make_async_copy(src, dst, lsem.at[at])
        started.start()
        return started

    cx = copy(tx, sh.at[0], core_peer)
    cg = copy(tg, sh.at[1], core_peer)
    load1 = local(w1_hbm, w1, 0)
    load2 = local(w2_hbm, w2, 1)

    def assemble(shard, other, buf):
        @pl.loop(0, 3)
        def _(j):
            cols = pl.ds(mul(j, 1024), 1024)
            mine, theirs = shard[:, cols].astype(F32), other[:, cols].astype(F32)
            first = c == 0
            zero = jnp.where(first, mine[0:24], theirs[24:48])
            one = jnp.where(first, theirs[0:24], mine[24:48])
            unit = jnp.concatenate([zero, one], axis=0).astype(BF16)
            buf[c, pl.ds(own_row, UNIT), cols] = unit

    own_row = pl.multiple_of(x * PAIR + zl * UNIT, UNIT)
    far_row = pl.multiple_of(x * PAIR + ozl * UNIT, UNIT)

    class Gather:
        def __init__(self, buf, cols_buf):
            self.buf, self.cols_buf = buf, cols_buf
            self.x, self.core, self.y, self.fwd, self.all = {}, {}, {}, {}, []

        def go(self, src, dst, device, landing=None):
            pair = copy(src, dst, device, landing)
            self.all.append(pair)
            return pair[0]

        def start_z(self):
            src = self.buf.at[c, pl.ds(own_row, UNIT)]
            self.z = self.go(src, src, zl_peer, self.buf.at[c, pl.ds(far_row, UNIT)])

        def start_x(self, part):
            for s in (1, 3, 2):
                from_x = ring(x, 4 - s)
                row = own_row if part == 0 else far_row
                land = pl.multiple_of(from_x * PAIR + (zl if part == 0 else ozl) * UNIT, UNIT)
                src = self.buf.at[c, pl.ds(row, UNIT)]
                self.x[s, part] = self.go(src, src, x_peer(s), self.buf.at[c, pl.ds(land, UNIT)])

        def start_core(self, s):
            if s:
                self.x[s, 0].wait_recv()
                self.x[s, 1].wait_recv()
            rows = pl.ds(mul(ring(x, 4 - s), PAIR), PAIR)
            src = self.buf.at[c, rows]
            self.core[s] = self.go(src, src, core_peer, self.buf.at[oc, rows])

        def start_y(self, s):
            self.core[s].wait_recv()
            row = mul(ring(x, 4 - s), PAIR)
            for r in (1, 3, 2):
                q, origin = ring(y, r), ring(y, 4 - r)
                cols = pl.ds(pl.multiple_of(lax.rem(q, 2) * QUARTER + c * BLOCK, BLOCK), BLOCK)
                src = self.buf.at[lax.div(q, 2), pl.ds(row, PAIR), cols]
                into = pl.ds(mul(c, BLOCK), BLOCK)
                self.y[r, s] = self.go(
                    src,
                    self.cols_buf.at[pl.ds(pl.multiple_of(y * ROWS + row, PAIR), PAIR), into],
                    y_peer(r),
                    self.cols_buf.at[pl.ds(pl.multiple_of(origin * ROWS + row, PAIR), PAIR), into],
                )

        def own_columns(self, at):
            src = self.buf.at[lax.div(y, 2), :, pl.ds(mul(lax.rem(y, 2), QUARTER), QUARTER)]
            return local(src, self.cols_buf.at[pl.ds(mul(y, ROWS), ROWS)], at)

        def forward(self, r):
            for s in (0, 1, 3, 2):
                self.y[r, s].wait_recv()
            rows = pl.ds(mul(ring(y, 4 - r), ROWS), ROWS)
            src = self.cols_buf.at[rows, pl.ds(mul(c, BLOCK), BLOCK)]
            self.fwd[r] = self.go(src, src, core_peer, self.cols_buf.at[rows, pl.ds(mul(oc, BLOCK), BLOCK)])

    gx, gg = Gather(xb, xc), Gather(gb, gc)
    cx[0].wait_recv()
    assemble(tx, sh.at[0], xb)
    gx.start_z()
    gx.start_x(0)
    cg[0].wait_recv()
    assemble(tg, sh.at[1], gb)
    gx.z.wait_recv()
    gx.start_x(1)
    gg.start_z()
    gx.start_core(0)
    gx.start_y(0)
    gx.start_core(1)
    gx.start_core(3)
    gg.start_x(0)
    gx.start_y(1)
    gx.start_y(3)
    gx.start_core(2)
    gg.z.wait_recv()
    gg.start_x(1)
    gg.start_core(0)
    gx.start_y(2)

    load1.wait()

    @pl.loop(0, 3)
    def _(n):
        cols = pl.ds(mul(n, 256), 256)
        acc[:, cols] = dot(xb[0], w1[0:HALF, cols]) + dot(xb[1], w1[HALF:D, cols])

    @pl.loop(0, 8)
    def _(i):
        rows = pl.ds(mul(i, UNIT), UNIT)
        u = acc[rows, :]
        t = jnp.tanh(root_coeff * (u + cubic_coeff * u * u * u))
        hb[rows, :] = (0.5 * u * (1.0 + t)).astype(BF16)
        acc[rows, :] = 0.5 * (1.0 + t) + 0.5 * u * (1.0 - t * t) * root_coeff * (
            1.0 + 3.0 * cubic_coeff * u * u
        )

    def transpose_out(into):
        for i in range(3):
            cols = pl.ds(pl.multiple_of(y * ROWS + i * 128, 128), 128)
            into[:, cols] = hb[i * 128 : (i + 1) * 128, :].astype(F32).T.astype(BF16)

    def share(into):
        pairs = {}
        cols = pl.ds(mul(y, ROWS), ROWS)
        for half in (0, 1):
            for r in (1, 3, 2):
                rows = pl.ds(half * ROWS, ROWS)
                src = into.at[rows, cols]
                land = into.at[rows, pl.ds(mul(ring(y, 4 - r), ROWS), ROWS)]
                pairs[r, half] = copy(src, src, y_peer(r), land)[0]
        return pairs

    transpose_out(ht)
    hts = share(ht)
    own_x = gx.own_columns(2)

    class Reduce:
        def __init__(self, op, buf, out_ref, product):
            self.op, self.buf, self.out_ref, self.product = op, buf, out_ref, product
            self.core, self.x = {}, {}

        def compute(self, half, j):
            @pl.loop(0, 2)
            def _(n):
                off = j * CHUNK + n * 512
                cols = pl.ds(pl.multiple_of(off, 512), 512)
                part = self.product(pl.multiple_of(half * HALF + off, 512), 512)
                self.buf[half, :, cols] = part.astype(BF16)

        def start_core(self):
            for j in range(3):
                cols = pl.ds(j * CHUNK, CHUNK)
                self.compute(oc, j)
                self.core[j] = copy(self.buf.at[oc, :, cols], rcore.at[:, cols], core_peer)[0]

        def start_x(self):
            for j in range(3):
                cols = pl.ds(j * CHUNK, CHUNK)
                self.compute(c, j)
                self.core[j].wait_recv()

                @pl.loop(0, 8)
                def _(i):
                    rows = pl.ds(mul(i, UNIT), UNIT)
                    both = self.buf[c, rows, cols].astype(F32) + rcore[rows, cols].astype(F32)
                    self.buf[c, rows, cols] = both.astype(BF16)

                for s in (1, 3, 2):
                    src = self.buf.at[c, pl.ds(mul(ring(x, s), PAIR), PAIR), cols]
                    self.x[s, j] = copy(src, rx.at[self.op, s - 1, :, cols], x_peer(s))[0]

        def start_z(self):
            for j in range(3):
                for s in (1, 3, 2):
                    self.x[s, j].wait_recv()

            @pl.loop(0, 12)
            def _(i):
                cols = pl.ds(mul(i, 256), 256)
                rows = pl.ds(mul(x, PAIR), PAIR)
                total = self.buf[c, rows, cols].astype(F32)
                for s in range(3):
                    total = total + rx[self.op, s, :, cols].astype(F32)
                self.buf[c, rows, cols] = total.astype(BF16)

            self.z = copy(self.buf.at[c, pl.ds(far_row, UNIT)], rz.at[self.op], zl_peer)[0]

        def start_last(self):
            self.z.wait_recv()

            @pl.loop(0, 6)
            def _(i):
                cols = pl.ds(mul(i, 512), 512)
                rows = pl.ds(own_row, UNIT)
                total = self.buf[c, rows, cols].astype(F32) + rz[self.op, :, cols].astype(F32)
                self.buf[c, rows, cols] = total.astype(BF16)

            self.last = copy(self.buf.at[c, pl.ds(own_row, UNIT)], rf.at[self.op], core_peer)[0]

        def finish(self):
            self.last.wait_recv()

            def rows_of(value):
                value = value.astype(F32)
                return jnp.where(c == 0, value[0:24], value[24:48]).astype(BF16)

            @pl.loop(0, 3)
            def _(j):
                cols = pl.ds(mul(j, CHUNK), CHUNK)
                mine = self.buf[c, pl.ds(own_row, UNIT), cols]
                theirs = rf[self.op, :, cols]
                self.out_ref[:, pl.ds(pl.multiple_of(c * HALF + j * CHUNK, CHUNK), CHUNK)] = rows_of(mine)
                self.out_ref[:, pl.ds(pl.multiple_of(oc * HALF + j * CHUNK, CHUNK), CHUNK)] = rows_of(theirs)

    load2.wait()
    red1 = Reduce(0, pb, out_o, lambda at, n: dot(hb[...], w2[:, pl.ds(at, n)]))
    red2 = Reduce(1, xb, tok_o, lambda at, n: dot_nt(hb[...], w1[pl.ds(at, n), :]))
    red1.start_core()
    gg.start_y(0)
    red1.start_x()
    pl.semaphore_signal(credit, inc=1, device_id=core_peer, device_id_type=MESH)

    gg.start_core(1)
    gg.start_core(3)
    gg.start_y(1)
    gg.start_y(3)
    gg.start_core(2)
    gg.start_y(2)
    own_g = gg.own_columns(3)

    @pl.loop(0, 3)
    def _(n):
        cols = pl.ds(mul(n, 256), 256)
        acc2[:, cols] = dot_nt(gb[0], w2[cols, 0:HALF]) + dot_nt(gb[1], w2[cols, HALF:D])

    @pl.loop(0, 8)
    def _(i):
        rows = pl.ds(mul(i, UNIT), UNIT)
        hb[rows, :] = (acc2[rows, :] * acc[rows, :]).astype(BF16)

    transpose_out(pt)
    pts = share(pt)
    for r in (1, 3, 2):
        gx.forward(r)
    own_x.wait()
    finish_sends(gx.all[:-3])
    pl.semaphore_wait(credit, 1)
    red2.start_core()
    red2.start_x()
    red1.start_z()

    def term(rows_ref, cols_ref, half, block, put):
        @pl.loop(0, 3)
        def _(n):
            cols = pl.ds(pl.multiple_of(block * BLOCK + n * 256, 256), 256)
            put(half, n, dot(rows_ref[half * ROWS : (half + 1) * ROWS, :], cols_ref[:, cols]).astype(BF16))

    for r in (1, 3, 2):
        gg.forward(r)
    red1.start_last()
    own_g.wait()
    for half in (0, 1):
        for r in (1, 3, 2):
            hts[r, half].wait_recv()
    for r in (1, 3, 2):
        gg.fwd[r].wait_recv()

    def put_w2(base):
        def put(half, n, value):
            cols = pl.ds(pl.multiple_of(base + n * 256, 256), 256)
            w2[half * ROWS : (half + 1) * ROWS, cols] = value

        return put

    def put_w1(base):
        def put(half, n, value):
            w1[base + half * ROWS : base + (half + 1) * ROWS, pl.ds(mul(n, 256), 256)] = value

        return put

    go_z = {}
    for half in (0, 1):
        rows = pl.ds(half * ROWS, ROWS)
        term(ht, gc, half, ozh, put_w2(0))
        go_z[half] = copy(w2.at[rows, 0:BLOCK], zr.at[0, rows], zh_peer)[0]
    for half in (0, 1):
        term(ht, gc, half, zh, put_w2(BLOCK))

    red2.start_z()
    red1.finish()
    for r in (1, 3, 2):
        gx.fwd[r].wait_recv()
    gi_z = {}
    for half in (0, 1):
        rows = pl.ds(half * ROWS, ROWS)
        for r in (1, 3, 2):
            pts[r, half].wait_recv()
        term(pt, xc, half, ozh, put_w1(0))
        gi_z[half] = copy(w1.at[rows], zr.at[1, rows], zh_peer)[0]
    for half in (0, 1):
        term(pt, xc, half, zh, put_w1(BLOCK))
    red2.start_last()

    for half in (0, 1):
        go_z[half].wait_recv()

    @pl.loop(0, 8)
    def _(i):
        rows = pl.ds(mul(i, PAIR), PAIR)
        total = w2[rows, BLOCK : 2 * BLOCK].astype(F32) + zr[0, rows, :].astype(F32)
        zr[0, rows, :] = (total * FACTOR).astype(BF16)

    store_o = local(zr.at[0], go_o, 4)
    red2.finish()
    for half in (0, 1):
        gi_z[half].wait_recv()
        for i in range(3):
            lo = half * ROWS + i * 128
            total = w1[BLOCK + lo : BLOCK + lo + 128, :].astype(F32) + zr[1, lo : lo + 128, :].astype(F32)
            w1[2 * BLOCK : 3 * BLOCK, lo : lo + 128] = (total * FACTOR).T.astype(BF16)
    store_i = local(w1.at[2 * BLOCK : 3 * BLOCK], gi_o, 5)
    store_o.wait()
    store_i.wait()
    for started in sent:
        if id(started) not in done:
            started.wait_send()


def fold(rows):
    return jnp.concatenate([rows[:, :HALF], rows[:, HALF:]], axis=0)


def shards(tokens, out_cotangent, weight_in, weight_out):
    any_space = pl.BlockSpec(memory_space=pl.ANY)
    vmem = pl.BlockSpec(memory_space=pltpu.VMEM)
    return pl.pallas_call(
        kernel,
        out_shape=(
            jax.ShapeDtypeStruct((24, D), BF16),
            jax.ShapeDtypeStruct((24, D), BF16),
            jax.ShapeDtypeStruct((BLOCK, FH), BF16),
            jax.ShapeDtypeStruct((FH, BLOCK), BF16),
        ),
        in_specs=[vmem, vmem, any_space, any_space],
        out_specs=(vmem, vmem, any_space, any_space),
        scratch_shapes=[
            pltpu.VMEM((D, FH), BF16),
            pltpu.VMEM((FH, D), BF16),
            pltpu.VMEM((2, ROWS, HALF), BF16),
            pltpu.VMEM((2, ROWS, HALF), BF16),
            pltpu.VMEM((2, ROWS, HALF), BF16),
            pltpu.VMEM((4 * ROWS, QUARTER), BF16),
            pltpu.VMEM((4 * ROWS, QUARTER), BF16),
            pltpu.VMEM((FH, 4 * ROWS), BF16),
            pltpu.VMEM((FH, 4 * ROWS), BF16),
            pltpu.VMEM((2, UNIT, HALF), BF16),
            pltpu.VMEM((ROWS, FH), F32),
            pltpu.VMEM((ROWS, FH), F32),
            pltpu.VMEM((ROWS, FH), BF16),
            pltpu.VMEM((ROWS, HALF), BF16),
            pltpu.VMEM((2, 3, PAIR, HALF), BF16),
            pltpu.VMEM((2, UNIT, HALF), BF16),
            pltpu.VMEM((2, UNIT, HALF), BF16),
            pltpu.VMEM((2, BLOCK, BLOCK), BF16),
            pltpu.SemaphoreType.DMA((8,)),
            pltpu.SemaphoreType.DMA((N_COPIES,)),
            pltpu.SemaphoreType.DMA((N_COPIES,)),
            pltpu.SemaphoreType.REGULAR,
        ],
        compiler_params=pltpu.CompilerParams(
            collective_id=0, has_side_effects=True, vmem_limit_bytes=64000 * 1024
        ),
        cost_estimate=pl.CostEstimate(flops=21743271936, bytes_accessed=24000000, transcendentals=294912),
    )(fold(tokens), fold(out_cotangent), weight_in, weight_out)


def solution(mesh):
    return jax.shard_map(
        shards,
        mesh=mesh,
        in_specs=(P(("dp", "mp"), None), P(("dp", "mp"), None), P(None, "mp"), P("mp", None)),
        out_specs=(P(("dp", "mp"), None), P(("dp", "mp"), None), P("dp", "mp"), P("mp", "dp")),
        check_vma=False,
    )
```

```python
import functools

import jax
import jax.numpy as jnp
from jax import lax
from jax.experimental import pallas as pl
from jax.experimental.pallas import tpu as pltpu
from jax.sharding import PartitionSpec as P

MESH = pl.DeviceIdType.MESH
BF16 = jnp.bfloat16
F32 = jnp.float32
D = 6144
HALF = 3072
QUARTER = 1536
BLOCK = 768
ROWS = 384
UNIT = 48
PAIR = 96
FH = 768
PART = 192
CHUNK = 1024
N_COPIES = 136
FACTOR = 3072.0**-0.5

root_coeff = 0.7978845608028654
cubic_coeff = 0.044715


def mul(value, step):
    return pl.multiple_of(value * step, step)


def dot(left, right):
    return jnp.dot(left, right, preferred_element_type=F32)


def dot_nt(left, right):
    return lax.dot_general(left, right, (((1,), (1,)), ((), ())), preferred_element_type=F32)


def kernel(
    tx, tg, w1_hbm, w2_hbm,
    out_o, tok_o, gi_o, go_o,
    w1, w2, xb, gb, pb, xc, gc, ht, pt, give, sh, acc, acc2, hb, pg, rcore, rx, rz, rf, zr,
    lsem, ssem, rsem, credit,
):
    dp, mp = lax.axis_index("dp"), lax.axis_index("mp")
    y, zh = lax.div(dp, 2), lax.rem(dp, 2)
    zl, x, c = lax.div(mp, 8), lax.rem(lax.div(mp, 2), 4), lax.rem(mp, 2)
    oc, ozl, ozh = 1 - c, 1 - zl, 1 - zh

    def ring(value, shift):
        return lax.rem(value + shift, 4)

    core_peer = (dp, zl * 8 + x * 2 + oc)
    zl_peer = (dp, ozl * 8 + x * 2 + c)
    zh_peer = (y * 2 + ozh, mp)

    def x_peer(shift):
        return (dp, zl * 8 + ring(x, shift) * 2 + c)

    def y_peer(shift):
        return (ring(y, shift) * 2 + zh, mp)

    counter = [0]
    sent, done = [], set()

    def copy(src, dst, device, landing=None):
        at = counter[0]
        counter[0] += 1
        started = pltpu.make_async_remote_copy(
            src_ref=src, dst_ref=dst, send_sem=ssem.at[at], recv_sem=rsem.at[at],
            device_id=device, device_id_type=MESH,
        )
        started.start()
        here = started
        if landing is not None:
            here = pltpu.make_async_remote_copy(
                src_ref=src, dst_ref=landing, send_sem=ssem.at[at], recv_sem=rsem.at[at],
                device_id=device, device_id_type=MESH,
            )
        sent.append(started)
        return here, started

    def finish_sends(pairs):
        for _, started in pairs:
            started.wait_send()
            done.add(id(started))

    barrier = pltpu.get_barrier_semaphore()
    peers = [core_peer, zl_peer, zh_peer] + [x_peer(s) for s in (1, 2, 3)] + [y_peer(s) for s in (1, 2, 3)]
    for peer in peers:
        pl.semaphore_signal(barrier, inc=1, device_id=peer, device_id_type=MESH)
    pl.semaphore_wait(barrier, len(peers))

    def local(src, dst, at):
        started = pltpu.make_async_copy(src, dst, lsem.at[at])
        started.start()
        return started

    def hand_over(shard, at):
        @pl.loop(0, 3)
        def _(j):
            theirs = shard[:, pl.ds(pl.multiple_of(oc * HALF + j * 1024, 1024), 1024)].astype(F32)
            padded = jnp.concatenate([theirs, jnp.zeros((8, 1024), F32)], axis=0)
            give[at, :, pl.ds(mul(j, 1024), 1024)] = padded.astype(BF16)

        return copy(give.at[at], sh.at[at], core_peer)

    cg = hand_over(tg, 1)
    cx = hand_over(tx, 0)
    load2 = local(w2_hbm, w2, 1)
    load1 = local(w1_hbm, w1, 0)

    def assemble(shard, other, buf):
        @pl.loop(0, 3)
        def _(j):
            cols = pl.ds(mul(j, 1024), 1024)
            mine = shard[:, pl.ds(pl.multiple_of(c * HALF + j * 1024, 1024), 1024)].astype(F32)
            theirs = other[:, cols].astype(F32)[0:24]
            first = c == 0
            zero = jnp.where(first, mine, theirs)
            one = jnp.where(first, theirs, mine)
            unit = jnp.concatenate([zero, one], axis=0).astype(BF16)
            buf[c, pl.ds(own_row, UNIT), cols] = unit

    own_row = pl.multiple_of(x * PAIR + zl * UNIT, UNIT)
    far_row = pl.multiple_of(x * PAIR + ozl * UNIT, UNIT)

    class Gather:
        def __init__(self, view):
            self.view = view
            self.x, self.core, self.all = {}, {}, []

        def go(self, src, dst, device, landing=None):
            pair = copy(src, dst, device, landing)
            self.all.append(pair)
            return pair[0]

        def unit(self, row):
            return self.view(c, pl.ds(row, UNIT))

        def start_z(self):
            self.z = self.go(self.unit(own_row), self.unit(own_row), zl_peer, self.unit(far_row))

        def start_x(self, part):
            for s in (1, 3):
                row = own_row if part == 0 else far_row
                land = pl.multiple_of(ring(x, 4 - s) * PAIR + (zl if part == 0 else ozl) * UNIT, UNIT)
                self.x[s, part] = self.go(self.unit(row), self.unit(row), x_peer(s), self.unit(land))

        def forward_x(self):
            across = ring(x, 2) * PAIR
            for s, part in ((1, 0), (3, 1)):
                self.x[s, part].wait_recv()
                off = (zl if part == 0 else ozl) * UNIT
                row = pl.multiple_of(ring(x, 4 - s) * PAIR + off, UNIT)
                land = self.unit(pl.multiple_of(across + off, UNIT))
                self.x[2, part] = self.go(self.unit(row), self.unit(row), x_peer(s), land)

        def start_core(self, s):
            if s == 1:
                self.x[1, 1].wait_recv()
            elif s == 3:
                self.x[3, 0].wait_recv()
            elif s == 2:
                self.x[s, 0].wait_recv()
                self.x[s, 1].wait_recv()
            rows = pl.ds(mul(ring(x, 4 - s), PAIR), PAIR)
            src = self.view(c, rows)
            self.core[s] = self.go(src, src, core_peer, self.view(oc, rows))

    def quarter(buf, q, rows):
        return buf.at[lax.div(q, 2), rows, pl.ds(pl.multiple_of(lax.rem(q, 2) * QUARTER + c * BLOCK, BLOCK), BLOCK)]

    g_y, g_fwd, x_y = {}, {}, {}

    def start_columns(s):
        gg.core[s].wait_recv()
        row = mul(ring(x, 4 - s), PAIR)
        into = pl.ds(mul(c, BLOCK), BLOCK)
        for r in (1, 3, 2):
            here = gc.at[pl.ds(pl.multiple_of(y * ROWS + row, PAIR), PAIR), into]
            land = gc.at[pl.ds(pl.multiple_of(ring(y, 4 - r) * ROWS + row, PAIR), PAIR), into]
            g_y[r, s] = gg.go(quarter(gb, ring(y, r), pl.ds(row, PAIR)), here, y_peer(r), land)

    def forward_columns(r):
        for s in (0, 1, 3, 2):
            g_y[r, s].wait_recv()
        rows = pl.ds(mul(ring(y, 4 - r), ROWS), ROWS)
        src = gc.at[rows, pl.ds(mul(c, BLOCK), BLOCK)]
        g_fwd[r] = copy(src, src, core_peer, gc.at[rows, pl.ds(mul(oc, BLOCK), BLOCK)])[0]

    def spread_tokens():
        rows = pl.ds(own_row, UNIT)
        for r in (1, 3, 2):
            here, land = xc.at[c, y, rows], xc.at[c, ring(y, 4 - r), rows]
            x_y[r] = copy(quarter(xb, ring(y, r), rows), here, y_peer(r), land)[0]
        return local(quarter(xb, y, rows), xc.at[c, y, rows], 2)

    gx = Gather(lambda half, rows: xb.at[half, rows])
    gg = Gather(lambda half, rows: gb.at[half, rows])
    gxc = Gather(lambda half, rows: xc.at[half, :, rows])
    cg[0].wait_recv()
    assemble(tg, sh.at[1], gb)
    gg.start_z()
    gg.start_x(0)
    cx[0].wait_recv()
    assemble(tx, sh.at[0], xb)
    gx.start_z()
    gg.z.wait_recv()
    gg.start_x(1)
    gg.start_core(0)
    gx.z.wait_recv()
    gx.start_core(0)
    start_columns(0)
    gg.forward_x()
    gx.start_x(0)
    gx.start_x(1)
    gx.core[0].wait_recv()
    own_x = spread_tokens()
    gg.start_core(1)
    gg.start_core(3)
    start_columns(1)
    start_columns(3)
    gg.start_core(2)
    start_columns(2)
    own_g = local(
        gb.at[lax.div(y, 2), :, pl.ds(mul(lax.rem(y, 2), QUARTER), QUARTER)], gc.at[pl.ds(mul(y, ROWS), ROWS)], 3
    )
    own_x.wait()
    for r in (1, 3, 2):
        x_y[r].wait_recv()
    gxc.start_z()

    load2.wait()

    @pl.loop(0, 3)
    def _(n):
        cols = pl.ds(mul(n, 256), 256)
        acc2[:, cols] = dot_nt(gb[0], w2[cols, 0:HALF]) + dot_nt(gb[1], w2[cols, HALF:D])

    gx.forward_x()
    gxc.start_x(0)
    gxc.z.wait_recv()
    gxc.start_x(1)
    gx.start_core(1)
    gx.start_core(3)
    gx.start_core(2)
    gxc.start_core(0)

    load1.wait()

    @pl.loop(0, 3)
    def _(n):
        cols = pl.ds(mul(n, 256), 256)
        acc[:, cols] = dot(xb[c], w1[pl.ds(mul(c, HALF), HALF), cols])

    for s in (1, 3, 2):
        gx.core[s].wait_recv()

    @pl.loop(0, 3)
    def _(n):
        cols = pl.ds(mul(n, 256), 256)
        acc[:, cols] += dot(xb[oc], w1[pl.ds(mul(oc, HALF), HALF), cols])

    @pl.loop(0, 8)
    def _(i):
        rows = pl.ds(mul(i, UNIT), UNIT)
        u = acc[rows, :]
        t = jnp.tanh(root_coeff * (u + cubic_coeff * u * u * u))
        hb[rows, :] = (0.5 * u * (1.0 + t)).astype(BF16)
        acc[rows, :] = 0.5 * (1.0 + t) + 0.5 * u * (1.0 - t * t) * root_coeff * (
            1.0 + 3.0 * cubic_coeff * u * u
        )

    def transpose_out(rows_ref, into):
        for i in range(3):
            cols = pl.ds(pl.multiple_of(y * ROWS + i * 128, 128), 128)
            into[:, cols] = rows_ref[i * 128 : (i + 1) * 128, :].astype(F32).T.astype(BF16)

    def share(into):
        pairs = {}
        cols = pl.ds(mul(y, ROWS), ROWS)
        for k in range(4):
            for r in (1, 3, 2):
                rows = pl.ds(k * PART, PART)
                src = into.at[rows, cols]
                land = into.at[rows, pl.ds(mul(ring(y, 4 - r), ROWS), ROWS)]
                pairs[r, k] = copy(src, src, y_peer(r), land)[0]
        return pairs

    transpose_out(hb, ht)
    hts = share(ht)

    @pl.loop(0, 8)
    def _(i):
        rows = pl.ds(mul(i, UNIT), UNIT)
        pg[rows, :] = (acc2[rows, :] * acc[rows, :]).astype(BF16)

    transpose_out(pg, pt)
    pts = share(pt)
    gxc.forward_x()
    for r in (1, 3, 2):
        forward_columns(r)

    class Reduce:
        def __init__(self, op, buf, out_ref, product):
            self.op, self.buf, self.out_ref, self.product = op, buf, out_ref, product
            self.core, self.x = {}, {}

        def compute(self, half, j):
            @pl.loop(0, 2)
            def _(n):
                off = j * CHUNK + n * 512
                cols = pl.ds(pl.multiple_of(off, 512), 512)
                part = self.product(pl.multiple_of(half * HALF + off, 512), 512)
                self.buf[half, :, cols] = part.astype(BF16)

        def start_core(self):
            for j in range(3):
                cols = pl.ds(j * CHUNK, CHUNK)
                self.compute(oc, j)
                self.core[j] = copy(self.buf.at[oc, :, cols], rcore.at[:, cols], core_peer)[0]

        def start_x(self):
            for j in range(3):
                cols = pl.ds(j * CHUNK, CHUNK)
                self.compute(c, j)
                self.core[j].wait_recv()

                @pl.loop(0, 8)
                def _(i):
                    rows = pl.ds(mul(i, UNIT), UNIT)
                    both = self.buf[c, rows, cols].astype(F32) + rcore[rows, cols].astype(F32)
                    self.buf[c, rows, cols] = both.astype(BF16)

                for slot, shift, to, part in ((0, 2, 1, 0), (1, 2, 3, 1), (2, 1, 1, 1), (3, 3, 3, 0)):
                    self.send(slot, j, shift, to, part)

        def send(self, slot, j, shift, to, part):
            cols = pl.ds(j * CHUNK, CHUNK)
            src = self.buf.at[c, self.rows(shift, part), cols]
            self.x[slot, j] = copy(src, rx.at[self.op, slot, :, cols], x_peer(to))[0]

        def rows(self, shift, part):
            return pl.ds(pl.multiple_of(ring(x, shift) * PAIR + part * UNIT, UNIT), UNIT)

        def relay(self, j):
            cols = pl.ds(j * CHUNK, CHUNK)
            for slot, to, part in ((0, 1, 0), (1, 3, 1)):
                self.x[slot, j].wait_recv()
                rows = self.rows(to, part)
                both = self.buf[c, rows, cols].astype(F32) + rx[self.op, slot, :, cols].astype(F32)
                self.buf[c, rows, cols] = both.astype(BF16)
                self.send(slot + 4, j, to, to, part)

        def start_z(self):
            for j in range(3):
                for slot in (2, 3, 4, 5):
                    self.x[slot, j].wait_recv()

            @pl.loop(0, 6)
            def _(i):
                cols = pl.ds(mul(i, 512), 512)
                for part, first, second in ((0, 3, 4), (1, 2, 5)):
                    rows = self.rows(0, part)
                    total = self.buf[c, rows, cols].astype(F32)
                    total = total + rx[self.op, first, :, cols].astype(F32)
                    total = total + rx[self.op, second, :, cols].astype(F32)
                    self.buf[c, rows, cols] = total.astype(BF16)

            self.z = copy(self.buf.at[c, pl.ds(far_row, UNIT)], rz.at[self.op], zl_peer)[0]

        def start_last(self):
            self.z.wait_recv()

            @pl.loop(0, 6)
            def _(i):
                cols = pl.ds(mul(i, 512), 512)
                rows = pl.ds(own_row, UNIT)
                total = self.buf[c, rows, cols].astype(F32) + rz[self.op, :, cols].astype(F32)
                self.buf[c, rows, cols] = total.astype(BF16)

            self.last = copy(self.buf.at[c, pl.ds(own_row, UNIT)], rf.at[self.op], core_peer)[0]

        def finish(self):
            self.last.wait_recv()

            def rows_of(value):
                value = value.astype(F32)
                return jnp.where(c == 0, value[0:24], value[24:48]).astype(BF16)

            @pl.loop(0, 3)
            def _(j):
                cols = pl.ds(mul(j, CHUNK), CHUNK)
                mine = self.buf[c, pl.ds(own_row, UNIT), cols]
                theirs = rf[self.op, :, cols]
                self.out_ref[:, pl.ds(pl.multiple_of(c * HALF + j * CHUNK, CHUNK), CHUNK)] = rows_of(mine)
                self.out_ref[:, pl.ds(pl.multiple_of(oc * HALF + j * CHUNK, CHUNK), CHUNK)] = rows_of(theirs)

    red1 = Reduce(0, pb, out_o, lambda at, n: dot(hb[...], w2[:, pl.ds(at, n)]))
    red2 = Reduce(1, gb, tok_o, lambda at, n: dot_nt(pg[...], w1[pl.ds(at, n), :]))
    def out_columns(block, n):
        return gc[:, pl.ds(pl.multiple_of(block * BLOCK + n * 256, 256), 256)]

    def in_columns(block, n):
        return xc[block, :, :, pl.ds(mul(n, 256), 256)].reshape(4 * ROWS, 256)

    def term(rows_ref, columns, rows, block, put):
        @pl.loop(0, 3)
        def _(n):
            put(rows, n, dot(rows_ref[rows, :], columns(block, n)).astype(BF16))

    def whole(rows_ref, columns, put):
        term(rows_ref, columns, slice(0, FH), zh, put)

    def put_w2(base):
        def put(rows, n, value):
            w2[rows, pl.ds(pl.multiple_of(base + n * 256, 256), 256)] = value

        return put

    def put_w1(base):
        def put(rows, n, value):
            w1[base + rows.start : base + rows.stop, pl.ds(mul(n, 256), 256)] = value

        return put

    go_z, gi_z = {}, {}

    def term_out(k):
        for r in (1, 3, 2):
            hts[r, k].wait_recv()
        rows = pl.ds(k * PART, PART)
        term(ht, out_columns, slice(k * PART, (k + 1) * PART), ozh, put_w2(0))
        go_z[k] = copy(w2.at[rows, 0:BLOCK], zr.at[0, rows], zh_peer)[0]

    def term_in(k):
        for r in (1, 3, 2):
            pts[r, k].wait_recv()
        rows = pl.ds(k * PART, PART)
        term(pt, in_columns, slice(k * PART, (k + 1) * PART), ozh, put_w1(0))
        gi_z[k] = copy(w1.at[rows], zr.at[1, rows], zh_peer)[0]

    red1.start_core()
    red1.start_x()
    gxc.start_core(1)
    gxc.start_core(3)
    pl.semaphore_signal(credit, inc=1, device_id=core_peer, device_id_type=MESH)
    for r in (1, 3, 2):
        g_fwd[r].wait_recv()
    own_g.wait()
    term_out(0)
    for j in range(3):
        red1.relay(j)
    finish_sends(gg.all)
    pl.semaphore_wait(credit, 1)
    red2.start_core()
    term_out(1)
    red2.start_x()
    term_out(2)
    gxc.start_core(2)
    term_out(3)
    red1.start_z()
    for j in range(3):
        red2.relay(j)
    for s in (0, 1, 3, 2):
        gxc.core[s].wait_recv()
    term_in(0)
    red1.start_last()
    whole(ht, out_columns, put_w2(BLOCK))
    term_in(1)
    red1.finish()
    term_in(2)
    red2.start_z()
    term_in(3)
    red2.start_last()
    whole(pt, in_columns, put_w1(BLOCK))

    for k in range(4):
        go_z[k].wait_recv()

    @pl.loop(0, 8)
    def _(i):
        rows = pl.ds(mul(i, PAIR), PAIR)
        total = w2[rows, BLOCK : 2 * BLOCK].astype(F32) + zr[0, rows, :].astype(F32)
        zr[0, rows, :] = (total * FACTOR).astype(BF16)

    store_o = local(zr.at[0], go_o, 4)
    red2.finish()
    for k in range(4):
        gi_z[k].wait_recv()
        if k % 2:
            for i in range(3):
                lo = (k // 2) * ROWS + i * 128
                total = w1[BLOCK + lo : BLOCK + lo + 128, :].astype(F32) + zr[1, lo : lo + 128, :].astype(F32)
                w1[2 * BLOCK : 3 * BLOCK, lo : lo + 128] = (total * FACTOR).T.astype(BF16)
    store_i = local(w1.at[2 * BLOCK : 3 * BLOCK], gi_o, 5)
    store_o.wait()
    store_i.wait()
    for started in sent:
        if id(started) not in done:
            started.wait_send()


def hand_out(*refs):
    for source, out in zip(refs[:4], refs[4:]):
        out[...] = source[...]


def shards(tokens, out_cotangent, weight_in, weight_out):
    any_space = pl.BlockSpec(memory_space=pl.ANY)
    vmem = pl.BlockSpec(memory_space=pltpu.VMEM)
    out_shape = (
        jax.ShapeDtypeStruct((24, D), BF16),
        jax.ShapeDtypeStruct((24, D), BF16),
        jax.ShapeDtypeStruct((BLOCK, FH), BF16),
        jax.ShapeDtypeStruct((FH, BLOCK), BF16),
    )
    results = pl.pallas_call(
        kernel,
        out_shape=out_shape,
        in_specs=[vmem, vmem, any_space, any_space],
        out_specs=(vmem, vmem, any_space, any_space),
        scratch_shapes=[
            pltpu.VMEM((D, FH), BF16),
            pltpu.VMEM((FH, D), BF16),
            pltpu.VMEM((2, ROWS, HALF), BF16),
            pltpu.VMEM((2, ROWS, HALF), BF16),
            pltpu.VMEM((2, ROWS, HALF), BF16),
            pltpu.VMEM((2, 4, ROWS, BLOCK), BF16),
            pltpu.VMEM((4 * ROWS, QUARTER), BF16),
            pltpu.VMEM((FH, 4 * ROWS), BF16),
            pltpu.VMEM((FH, 4 * ROWS), BF16),
            pltpu.VMEM((2, 32, HALF), BF16),
            pltpu.VMEM((2, 32, HALF), BF16),
            pltpu.VMEM((ROWS, FH), F32),
            pltpu.VMEM((ROWS, FH), F32),
            pltpu.VMEM((ROWS, FH), BF16),
            pltpu.VMEM((ROWS, FH), BF16),
            pltpu.VMEM((ROWS, HALF), BF16),
            pltpu.VMEM((2, 6, UNIT, HALF), BF16),
            pltpu.VMEM((2, UNIT, HALF), BF16),
            pltpu.VMEM((2, UNIT, HALF), BF16),
            pltpu.VMEM((2, BLOCK, BLOCK), BF16),
            pltpu.SemaphoreType.DMA((8,)),
            pltpu.SemaphoreType.DMA((N_COPIES,)),
            pltpu.SemaphoreType.DMA((N_COPIES,)),
            pltpu.SemaphoreType.REGULAR,
        ],
        compiler_params=pltpu.CompilerParams(
            collective_id=0, has_side_effects=True, vmem_limit_bytes=64000 * 1024
        ),
        cost_estimate=pl.CostEstimate(flops=21743271936, bytes_accessed=24000000, transcendentals=294912),
    )(tokens, out_cotangent, weight_in, weight_out)
    blocks = [pl.BlockSpec((24, D // 4), lambda i: (0, i))] * 2 + [pl.BlockSpec((FH // 4, FH), lambda i: (i, 0))] * 2
    return pl.pallas_call(
        hand_out,
        out_shape=out_shape,
        grid=(4,),
        in_specs=blocks,
        out_specs=tuple(blocks),
        compiler_params=pltpu.CompilerParams(vmem_limit_bytes=64000 * 1024),
    )(*results)


def solution(mesh):
    return jax.shard_map(
        shards,
        mesh=mesh,
        in_specs=(P(("dp", "mp"), None), P(("dp", "mp"), None), P(None, "mp"), P("mp", None)),
        out_specs=(P(("dp", "mp"), None), P(("dp", "mp"), None), P("dp", "mp"), P("mp", "dp")),
        check_vma=False,
    )
```

```python
import functools

import jax
import jax.numpy as jnp
from jax import lax
from jax.experimental import pallas as pl
from jax.experimental.pallas import tpu as pltpu
from jax.sharding import PartitionSpec as P

MESH = pl.DeviceIdType.MESH
BF16 = jnp.bfloat16
F32 = jnp.float32
D = 6144
HALF = 3072
QUARTER = 1536
BLOCK = 768
ROWS = 384
UNIT = 48
PAIR = 96
FH = 768
PART = 192
CHUNK = 1024
N_COPIES = 144
FACTOR = 3072.0**-0.5

root_coeff = 0.7978845608028654
cubic_coeff = 0.044715


def mul(value, step):
    return pl.multiple_of(value * step, step)


def dot(left, right):
    return jnp.dot(left, right, preferred_element_type=F32)


def dot_nt(left, right):
    return lax.dot_general(left, right, (((1,), (1,)), ((), ())), preferred_element_type=F32)


def kernel(
    tx, tg, w1_hbm, w2_hbm,
    out_o, tok_o, gi_o, go_o,
    w1, w2, xb, gb, pb, xc, gc, ht, pt, give, sh, acc, acc2, hb, pg, rcore, rx, rz, rf, zr,
    lsem, ssem, rsem, credit,
):
    dp, mp = lax.axis_index("dp"), lax.axis_index("mp")
    y, zh = lax.div(dp, 2), lax.rem(dp, 2)
    zl, x, c = lax.div(mp, 8), lax.rem(lax.div(mp, 2), 4), lax.rem(mp, 2)
    oc, ozl, ozh = 1 - c, 1 - zl, 1 - zh

    def ring(value, shift):
        return lax.rem(value + shift, 4)

    core_peer = (dp, zl * 8 + x * 2 + oc)
    zl_peer = (dp, ozl * 8 + x * 2 + c)
    zh_peer = (y * 2 + ozh, mp)

    def x_peer(shift):
        return (dp, zl * 8 + ring(x, shift) * 2 + c)

    def y_peer(shift):
        return (ring(y, shift) * 2 + zh, mp)

    counter = [0]
    sent, done = [], set()

    def copy(src, dst, device, landing=None):
        at = counter[0]
        counter[0] += 1
        started = pltpu.make_async_remote_copy(
            src_ref=src, dst_ref=dst, send_sem=ssem.at[at], recv_sem=rsem.at[at],
            device_id=device, device_id_type=MESH,
        )
        started.start()
        here = started
        if landing is not None:
            here = pltpu.make_async_remote_copy(
                src_ref=src, dst_ref=landing, send_sem=ssem.at[at], recv_sem=rsem.at[at],
                device_id=device, device_id_type=MESH,
            )
        sent.append(started)
        return here, started

    def finish_sends(pairs):
        for _, started in pairs:
            started.wait_send()
            done.add(id(started))

    barrier = pltpu.get_barrier_semaphore()
    peers = [core_peer, zl_peer, zh_peer] + [x_peer(s) for s in (1, 2, 3)] + [y_peer(s) for s in (1, 2, 3)]
    for peer in peers:
        pl.semaphore_signal(barrier, inc=1, device_id=peer, device_id_type=MESH)
    pl.semaphore_wait(barrier, len(peers))

    def local(src, dst, at):
        started = pltpu.make_async_copy(src, dst, lsem.at[at])
        started.start()
        return started

    def hand_over(shard, at):
        @pl.loop(0, 3)
        def _(j):
            theirs = shard[:, pl.ds(pl.multiple_of(oc * HALF + j * 1024, 1024), 1024)].astype(F32)
            padded = jnp.concatenate([theirs, jnp.zeros((8, 1024), F32)], axis=0)
            give[at, :, pl.ds(mul(j, 1024), 1024)] = padded.astype(BF16)

        return copy(give.at[at], sh.at[at], core_peer)

    cg = hand_over(tg, 1)
    cx = hand_over(tx, 0)
    load2 = local(w2_hbm, w2, 1)
    load1 = local(w1_hbm, w1, 0)

    def assemble(shard, other, buf):
        @pl.loop(0, 3)
        def _(j):
            cols = pl.ds(mul(j, 1024), 1024)
            mine = shard[:, pl.ds(pl.multiple_of(c * HALF + j * 1024, 1024), 1024)].astype(F32)
            theirs = other[:, cols].astype(F32)[0:24]
            first = c == 0
            zero = jnp.where(first, mine, theirs)
            one = jnp.where(first, theirs, mine)
            unit = jnp.concatenate([zero, one], axis=0).astype(BF16)
            buf[c, pl.ds(own_row, UNIT), cols] = unit

    own_row = pl.multiple_of(x * PAIR + zl * UNIT, UNIT)
    far_row = pl.multiple_of(x * PAIR + ozl * UNIT, UNIT)

    class Gather:
        def __init__(self, view):
            self.view = view
            self.x, self.core, self.all = {}, {}, []

        def go(self, src, dst, device, landing=None):
            pair = copy(src, dst, device, landing)
            self.all.append(pair)
            return pair[0]

        def unit(self, shift, far, cols=None):
            row = pl.multiple_of(ring(x, shift) * PAIR + (ozl if far else zl) * UNIT, UNIT)
            return self.view(c, pl.ds(row, UNIT), cols)

        def send(self, shift, far, device, land_shift, land_far, cols=None):
            src = self.unit(shift, far, cols)
            return self.go(src, src, device, self.unit(land_shift, land_far, cols))

        def start_z(self):
            self.z = self.send(0, 0, zl_peer, 0, 1)

        def start_x0(self):
            for s in (1, 3):
                self.x[s, 0] = self.send(0, 0, x_peer(s), 4 - s, 0)

        def start_x1(self):
            self.z.wait_recv()
            self.x[3, 1] = self.send(0, 1, x_peer(3), 1, 1)

        def middle(self):
            self.x[1, 0].wait_recv()
            self.x[2, 0] = self.send(3, 0, x_peer(1), 2, 0)
            self.z2 = self.send(3, 0, zl_peer, 3, 1)

        def late(self):
            self.z2.wait_recv()
            self.x[2, 1] = self.send(3, 1, x_peer(1), 2, 1, 0)
            self.x[3, 1].wait_recv()
            self.x[2, 2] = self.send(1, 1, x_peer(3), 2, 1, 1)

        def start_core(self, s):
            if s == 3:
                self.x[3, 0].wait_recv()
            elif s == 2:
                for part in range(3):
                    self.x[2, part].wait_recv()
            rows = pl.ds(mul(ring(x, 4 - s), PAIR), PAIR)
            src = self.view(c, rows)
            self.core[s] = self.go(src, src, core_peer, self.view(oc, rows))

    def quarter(buf, q, rows):
        return buf.at[lax.div(q, 2), rows, pl.ds(pl.multiple_of(lax.rem(q, 2) * QUARTER + c * BLOCK, BLOCK), BLOCK)]

    g_y, g_fwd, x_y = {}, {}, {}

    def start_columns(s):
        gg.core[s].wait_recv()
        row = mul(ring(x, 4 - s), PAIR)
        into = pl.ds(mul(c, BLOCK), BLOCK)
        for r in (1, 3, 2):
            here = gc.at[pl.ds(pl.multiple_of(y * ROWS + row, PAIR), PAIR), into]
            land = gc.at[pl.ds(pl.multiple_of(ring(y, 4 - r) * ROWS + row, PAIR), PAIR), into]
            g_y[r, s] = gg.go(quarter(gb, ring(y, r), pl.ds(row, PAIR)), here, y_peer(r), land)

    def forward_columns(r):
        for s in (0, 1, 3, 2):
            g_y[r, s].wait_recv()
        rows = pl.ds(mul(ring(y, 4 - r), ROWS), ROWS)
        src = gc.at[rows, pl.ds(mul(c, BLOCK), BLOCK)]
        g_fwd[r] = copy(src, src, core_peer, gc.at[rows, pl.ds(mul(oc, BLOCK), BLOCK)])[0]

    def spread_tokens():
        rows = pl.ds(own_row, UNIT)
        for r in (1, 3, 2):
            here, land = xc.at[c, y, rows], xc.at[c, ring(y, 4 - r), rows]
            x_y[r] = gx.go(quarter(xb, ring(y, r), rows), here, y_peer(r), land)
        return local(quarter(xb, y, rows), xc.at[c, y, rows], 2)

    def rows_view(buf):
        def view(half, rows, cols=None):
            return buf.at[half, rows] if cols is None else buf.at[half, rows, pl.ds(cols * QUARTER, QUARTER)]

        return view

    def columns_view(half, rows, cols=None):
        return xc.at[half, :, rows] if cols is None else xc.at[half, :, rows, pl.ds(cols * ROWS, ROWS)]

    gx, gg, gxc = Gather(rows_view(xb)), Gather(rows_view(gb)), Gather(columns_view)
    cg[0].wait_recv()
    assemble(tg, sh.at[1], gb)
    gg.start_z()
    gg.start_x0()
    cx[0].wait_recv()
    assemble(tx, sh.at[0], xb)
    gg.start_x1()
    gg.start_core(0)
    gg.middle()
    gx.start_z()
    gx.start_x0()
    start_columns(0)
    gg.late()
    gg.start_core(1)
    gg.start_core(3)
    gx.start_x1()
    gx.start_core(0)
    start_columns(1)
    start_columns(3)
    gx.middle()
    gx.core[0].wait_recv()
    own_x = spread_tokens()
    gg.start_core(2)
    start_columns(2)
    own_g = local(
        gb.at[lax.div(y, 2), :, pl.ds(mul(lax.rem(y, 2), QUARTER), QUARTER)], gc.at[pl.ds(mul(y, ROWS), ROWS)], 3
    )

    load2.wait()

    @pl.loop(0, 3)
    def _(n):
        cols = pl.ds(mul(n, 256), 256)
        acc2[:, cols] = dot_nt(gb[0], w2[cols, 0:HALF]) + dot_nt(gb[1], w2[cols, HALF:D])

    gx.late()
    own_x.wait()
    for r in (1, 3, 2):
        x_y[r].wait_recv()
    gxc.start_z()
    gxc.start_x0()
    gx.start_core(1)
    gx.start_core(3)
    gx.start_core(2)

    load1.wait()

    @pl.loop(0, 3)
    def _(n):
        cols = pl.ds(mul(n, 256), 256)
        acc[:, cols] = dot(xb[c], w1[pl.ds(mul(c, HALF), HALF), cols])

    for s in (1, 3, 2):
        gx.core[s].wait_recv()

    @pl.loop(0, 3)
    def _(n):
        cols = pl.ds(mul(n, 256), 256)
        acc[:, cols] += dot(xb[oc], w1[pl.ds(mul(oc, HALF), HALF), cols])

    @pl.loop(0, 8)
    def _(i):
        rows = pl.ds(mul(i, UNIT), UNIT)
        u = acc[rows, :]
        t = jnp.tanh(root_coeff * (u + cubic_coeff * u * u * u))
        hb[rows, :] = (0.5 * u * (1.0 + t)).astype(BF16)
        acc[rows, :] = 0.5 * (1.0 + t) + 0.5 * u * (1.0 - t * t) * root_coeff * (
            1.0 + 3.0 * cubic_coeff * u * u
        )

    def transpose_out(rows_ref, into):
        for i in range(3):
            cols = pl.ds(pl.multiple_of(y * ROWS + i * 128, 128), 128)
            into[:, cols] = rows_ref[i * 128 : (i + 1) * 128, :].astype(F32).T.astype(BF16)

    def share(into):
        pairs = {}
        cols = pl.ds(mul(y, ROWS), ROWS)
        for k in range(4):
            for r in (1, 3, 2):
                rows = pl.ds(k * PART, PART)
                src = into.at[rows, cols]
                land = into.at[rows, pl.ds(mul(ring(y, 4 - r), ROWS), ROWS)]
                pairs[r, k] = copy(src, src, y_peer(r), land)[0]
        return pairs

    transpose_out(hb, ht)
    hts = share(ht)
    gxc.start_x1()
    gxc.start_core(0)

    @pl.loop(0, 8)
    def _(i):
        rows = pl.ds(mul(i, UNIT), UNIT)
        pg[rows, :] = (acc2[rows, :] * acc[rows, :]).astype(BF16)

    transpose_out(pg, pt)
    pts = share(pt)
    gxc.middle()
    for r in (1, 3, 2):
        forward_columns(r)

    class Reduce:
        def __init__(self, op, buf, out_ref, product):
            self.op, self.buf, self.out_ref, self.product = op, buf, out_ref, product
            self.core, self.x = {}, {}

        def compute(self, half, j):
            @pl.loop(0, 2)
            def _(n):
                off = j * CHUNK + n * 512
                cols = pl.ds(pl.multiple_of(off, 512), 512)
                part = self.product(pl.multiple_of(half * HALF + off, 512), 512)
                self.buf[half, :, cols] = part.astype(BF16)

        def start_core(self):
            for j in range(3):
                cols = pl.ds(j * CHUNK, CHUNK)
                self.compute(oc, j)
                self.core[j] = copy(self.buf.at[oc, :, cols], rcore.at[:, cols], core_peer)[0]

        def start_x(self):
            for j in range(3):
                cols = pl.ds(j * CHUNK, CHUNK)
                self.compute(c, j)
                self.core[j].wait_recv()

                @pl.loop(0, 8)
                def _(i):
                    rows = pl.ds(mul(i, UNIT), UNIT)
                    both = self.buf[c, rows, cols].astype(F32) + rcore[rows, cols].astype(F32)
                    self.buf[c, rows, cols] = both.astype(BF16)

                for slot, shift, to, part in ((0, 2, 1, 0), (1, 2, 3, 1), (2, 1, 1, 1), (3, 3, 3, 0)):
                    self.send(slot, j, shift, to, part)

        def send(self, slot, j, shift, to, part):
            cols = pl.ds(j * CHUNK, CHUNK)
            src = self.buf.at[c, self.rows(shift, part), cols]
            self.x[slot, j] = copy(src, rx.at[self.op, slot, :, cols], x_peer(to))[0]

        def rows(self, shift, part):
            return pl.ds(pl.multiple_of(ring(x, shift) * PAIR + part * UNIT, UNIT), UNIT)

        def relay(self, j):
            cols = pl.ds(j * CHUNK, CHUNK)
            for slot, to, part in ((0, 1, 0), (1, 3, 1)):
                self.x[slot, j].wait_recv()
                rows = self.rows(to, part)
                both = self.buf[c, rows, cols].astype(F32) + rx[self.op, slot, :, cols].astype(F32)
                self.buf[c, rows, cols] = both.astype(BF16)
                self.send(slot + 4, j, to, to, part)

        def start_z(self):
            for j in range(3):
                for slot in (2, 3, 4, 5):
                    self.x[slot, j].wait_recv()

            @pl.loop(0, 6)
            def _(i):
                cols = pl.ds(mul(i, 512), 512)
                for part, first, second in ((0, 3, 4), (1, 2, 5)):
                    rows = self.rows(0, part)
                    total = self.buf[c, rows, cols].astype(F32)
                    total = total + rx[self.op, first, :, cols].astype(F32)
                    total = total + rx[self.op, second, :, cols].astype(F32)
                    self.buf[c, rows, cols] = total.astype(BF16)

            self.z = copy(self.buf.at[c, pl.ds(far_row, UNIT)], rz.at[self.op], zl_peer)[0]

        def start_last(self):
            self.z.wait_recv()

            @pl.loop(0, 6)
            def _(i):
                cols = pl.ds(mul(i, 512), 512)
                rows = pl.ds(own_row, UNIT)
                total = self.buf[c, rows, cols].astype(F32) + rz[self.op, :, cols].astype(F32)
                self.buf[c, rows, cols] = total.astype(BF16)

            self.last = copy(self.buf.at[c, pl.ds(own_row, UNIT)], rf.at[self.op], core_peer)[0]

        def finish(self):
            self.last.wait_recv()

            def rows_of(value):
                value = value.astype(F32)
                return jnp.where(c == 0, value[0:24], value[24:48]).astype(BF16)

            @pl.loop(0, 3)
            def _(j):
                cols = pl.ds(mul(j, CHUNK), CHUNK)
                mine = self.buf[c, pl.ds(own_row, UNIT), cols]
                theirs = rf[self.op, :, cols]
                self.out_ref[:, pl.ds(pl.multiple_of(c * HALF + j * CHUNK, CHUNK), CHUNK)] = rows_of(mine)
                self.out_ref[:, pl.ds(pl.multiple_of(oc * HALF + j * CHUNK, CHUNK), CHUNK)] = rows_of(theirs)

    red1 = Reduce(0, pb, out_o, lambda at, n: dot(hb[...], w2[:, pl.ds(at, n)]))
    red2 = Reduce(1, gb, tok_o, lambda at, n: dot_nt(pg[...], w1[pl.ds(at, n), :]))
    def out_columns(block, n):
        return gc[:, pl.ds(pl.multiple_of(block * BLOCK + n * 256, 256), 256)]

    def in_columns(block, n):
        return xc[block, :, :, pl.ds(mul(n, 256), 256)].reshape(4 * ROWS, 256)

    def term(rows_ref, columns, rows, block, put):
        @pl.loop(0, 3)
        def _(n):
            put(rows, n, dot(rows_ref[rows, :], columns(block, n)).astype(BF16))

    def whole(rows_ref, columns, put):
        term(rows_ref, columns, slice(0, FH), zh, put)

    def put_w2(base):
        def put(rows, n, value):
            w2[rows, pl.ds(pl.multiple_of(base + n * 256, 256), 256)] = value

        return put

    def put_w1(base):
        def put(rows, n, value):
            w1[base + rows.start : base + rows.stop, pl.ds(mul(n, 256), 256)] = value

        return put

    go_z, gi_z = {}, {}

    def term_out(k):
        for r in (1, 3, 2):
            hts[r, k].wait_recv()
        rows = pl.ds(k * PART, PART)

        def put_xb(_, n, value):
            xb[0, 0:PART, pl.ds(pl.multiple_of(k * BLOCK + n * 256, 256), 256)] = value

        term(ht, out_columns, slice(k * PART, (k + 1) * PART), ozh, put_xb)
        go_z[k] = copy(xb.at[0, 0:PART, k * BLOCK : (k + 1) * BLOCK], zr.at[0, rows], zh_peer)[0]

    def term_in(k):
        for r in (1, 3, 2):
            pts[r, k].wait_recv()
        rows = pl.ds(k * PART, PART)
        term(pt, in_columns, slice(k * PART, (k + 1) * PART), ozh, put_w1(0))
        gi_z[k] = copy(w1.at[rows], zr.at[1, rows], zh_peer)[0]

    red1.start_core()
    for r in (1, 3, 2):
        g_fwd[r].wait_recv()
    own_g.wait()
    finish_sends(gx.all)
    term_out(0)
    gxc.late()
    red1.start_x()
    pl.semaphore_signal(credit, inc=1, device_id=core_peer, device_id_type=MESH)
    term_out(1)
    gxc.start_core(1)
    gxc.start_core(3)
    finish_sends(gg.all)
    pl.semaphore_wait(credit, 1)
    red2.start_core()
    red2.start_x()
    red1.relay(0)
    term_out(2)
    red1.relay(1)
    gxc.start_core(2)
    red1.relay(2)
    term_out(3)
    whole(ht, out_columns, put_w2(BLOCK))
    for s in (0, 1, 3, 2):
        gxc.core[s].wait_recv()
    term_in(0)
    red1.start_z()
    red2.relay(0)
    term_in(1)
    red1.start_last()
    red2.relay(1)
    red2.relay(2)
    term_in(2)
    red1.finish()
    term_in(3)
    red2.start_z()
    whole(pt, in_columns, put_w1(BLOCK))
    red2.start_last()

    for k in range(4):
        go_z[k].wait_recv()

    @pl.loop(0, 8)
    def _(i):
        rows = pl.ds(mul(i, PAIR), PAIR)
        total = w2[rows, BLOCK : 2 * BLOCK].astype(F32) + zr[0, rows, :].astype(F32)
        zr[0, rows, :] = (total * FACTOR).astype(BF16)

    store_o = local(zr.at[0], go_o, 4)
    red2.finish()
    for k in range(4):
        gi_z[k].wait_recv()
        if k % 2:
            for i in range(3):
                lo = (k // 2) * ROWS + i * 128
                total = w1[BLOCK + lo : BLOCK + lo + 128, :].astype(F32) + zr[1, lo : lo + 128, :].astype(F32)
                w1[2 * BLOCK : 3 * BLOCK, lo : lo + 128] = (total * FACTOR).T.astype(BF16)
    store_i = local(w1.at[2 * BLOCK : 3 * BLOCK], gi_o, 5)
    store_o.wait()
    store_i.wait()
    for started in sent:
        if id(started) not in done:
            started.wait_send()


def hand_out(*refs):
    for source, out in zip(refs[:4], refs[4:]):
        out[...] = source[...]


def shards(tokens, out_cotangent, weight_in, weight_out):
    any_space = pl.BlockSpec(memory_space=pl.ANY)
    vmem = pl.BlockSpec(memory_space=pltpu.VMEM)
    out_shape = (
        jax.ShapeDtypeStruct((24, D), BF16),
        jax.ShapeDtypeStruct((24, D), BF16),
        jax.ShapeDtypeStruct((BLOCK, FH), BF16),
        jax.ShapeDtypeStruct((FH, BLOCK), BF16),
    )
    results = pl.pallas_call(
        kernel,
        out_shape=out_shape,
        in_specs=[vmem, vmem, any_space, any_space],
        out_specs=(vmem, vmem, any_space, any_space),
        scratch_shapes=[
            pltpu.VMEM((D, FH), BF16),
            pltpu.VMEM((FH, D), BF16),
            pltpu.VMEM((2, ROWS, HALF), BF16),
            pltpu.VMEM((2, ROWS, HALF), BF16),
            pltpu.VMEM((2, ROWS, HALF), BF16),
            pltpu.VMEM((2, 4, ROWS, BLOCK), BF16),
            pltpu.VMEM((4 * ROWS, QUARTER), BF16),
            pltpu.VMEM((FH, 4 * ROWS), BF16),
            pltpu.VMEM((FH, 4 * ROWS), BF16),
            pltpu.VMEM((2, 32, HALF), BF16),
            pltpu.VMEM((2, 32, HALF), BF16),
            pltpu.VMEM((ROWS, FH), F32),
            pltpu.VMEM((ROWS, FH), F32),
            pltpu.VMEM((ROWS, FH), BF16),
            pltpu.VMEM((ROWS, FH), BF16),
            pltpu.VMEM((ROWS, HALF), BF16),
            pltpu.VMEM((2, 6, UNIT, HALF), BF16),
            pltpu.VMEM((2, UNIT, HALF), BF16),
            pltpu.VMEM((2, UNIT, HALF), BF16),
            pltpu.VMEM((2, BLOCK, BLOCK), BF16),
            pltpu.SemaphoreType.DMA((8,)),
            pltpu.SemaphoreType.DMA((N_COPIES,)),
            pltpu.SemaphoreType.DMA((N_COPIES,)),
            pltpu.SemaphoreType.REGULAR,
        ],
        compiler_params=pltpu.CompilerParams(
            collective_id=0, has_side_effects=True, vmem_limit_bytes=64000 * 1024
        ),
        cost_estimate=pl.CostEstimate(flops=21743271936, bytes_accessed=24000000, transcendentals=294912),
    )(tokens, out_cotangent, weight_in, weight_out)
    blocks = [pl.BlockSpec((24, D // 4), lambda i: (0, i))] * 2 + [pl.BlockSpec((FH // 4, FH), lambda i: (i, 0))] * 2
    return pl.pallas_call(
        hand_out,
        out_shape=out_shape,
        grid=(4,),
        in_specs=blocks,
        out_specs=tuple(blocks),
        compiler_params=pltpu.CompilerParams(vmem_limit_bytes=64000 * 1024),
    )(*results)


def solution(mesh):
    return jax.shard_map(
        shards,
        mesh=mesh,
        in_specs=(P(("dp", "mp"), None), P(("dp", "mp"), None), P(None, "mp"), P("mp", None)),
        out_specs=(P(("dp", "mp"), None), P(("dp", "mp"), None), P("dp", "mp"), P("mp", "dp")),
        check_vma=False,
    )
```

```python
import functools

import jax
import jax.numpy as jnp
from jax import lax
from jax.experimental import pallas as pl
from jax.experimental.pallas import tpu as pltpu
from jax.sharding import PartitionSpec as P

MESH = pl.DeviceIdType.MESH
BF16 = jnp.bfloat16
F32 = jnp.float32
D = 6144
HALF = 3072
QUARTER = 1536
BLOCK = 768
ROWS = 384
UNIT = 48
PAIR = 96
FH = 768
PART = 192
CHUNK = 1024
N_COPIES = 144
FACTOR = 3072.0**-0.5

root_coeff = 0.7978845608028654
cubic_coeff = 0.044715


def mul(value, step):
    return pl.multiple_of(value * step, step)


def dot(left, right):
    return jnp.dot(left, right, preferred_element_type=F32)


def dot_nt(left, right):
    return lax.dot_general(left, right, (((1,), (1,)), ((), ())), preferred_element_type=F32)


def kernel(
    tx, tg, w1_hbm, w2_hbm,
    out_o, tok_o, gi_o, go_o,
    w1, w2, xb, gb, pb, xc, gc, ht, pt, give, sh, acc, acc2, hb, pg, rcore, rx, rz, rf, zr,
    lsem, ssem, rsem, credit,
):
    dp, mp = lax.axis_index("dp"), lax.axis_index("mp")
    y, zh = lax.div(dp, 2), lax.rem(dp, 2)
    zl, x, c = lax.div(mp, 8), lax.rem(lax.div(mp, 2), 4), lax.rem(mp, 2)
    oc, ozl, ozh = 1 - c, 1 - zl, 1 - zh

    def ring(value, shift):
        return lax.rem(value + shift, 4)

    core_peer = (dp, zl * 8 + x * 2 + oc)
    zl_peer = (dp, ozl * 8 + x * 2 + c)
    zh_peer = (y * 2 + ozh, mp)

    def x_peer(shift):
        return (dp, zl * 8 + ring(x, shift) * 2 + c)

    def y_peer(shift):
        return (ring(y, shift) * 2 + zh, mp)

    counter = [0]
    sent, done = [], set()

    def copy(src, dst, device, landing=None):
        at = counter[0]
        counter[0] += 1
        started = pltpu.make_async_remote_copy(
            src_ref=src, dst_ref=dst, send_sem=ssem.at[at], recv_sem=rsem.at[at],
            device_id=device, device_id_type=MESH,
        )
        started.start()
        here = started
        if landing is not None:
            here = pltpu.make_async_remote_copy(
                src_ref=src, dst_ref=landing, send_sem=ssem.at[at], recv_sem=rsem.at[at],
                device_id=device, device_id_type=MESH,
            )
        sent.append(started)
        return here, started

    def finish_sends(pairs):
        for _, started in pairs:
            started.wait_send()
            done.add(id(started))

    barrier = pltpu.get_barrier_semaphore()
    peers = [core_peer, zl_peer, zh_peer] + [x_peer(s) for s in (1, 2, 3)] + [y_peer(s) for s in (1, 2, 3)]
    for peer in peers:
        pl.semaphore_signal(barrier, inc=1, device_id=peer, device_id_type=MESH)
    pl.semaphore_wait(barrier, len(peers))

    def local(src, dst, at):
        started = pltpu.make_async_copy(src, dst, lsem.at[at])
        started.start()
        return started

    def hand_over(shard, at):
        @pl.loop(0, 3)
        def _(j):
            theirs = shard[:, pl.ds(pl.multiple_of(oc * HALF + j * 1024, 1024), 1024)].astype(F32)
            padded = jnp.concatenate([theirs, jnp.zeros((8, 1024), F32)], axis=0)
            give[at, :, pl.ds(mul(j, 1024), 1024)] = padded.astype(BF16)

        return copy(give.at[at], sh.at[at], core_peer)

    cg = hand_over(tg, 1)
    cx = hand_over(tx, 0)
    load2 = local(w2_hbm, w2, 1)
    load1 = local(w1_hbm, w1, 0)

    def assemble(shard, other, buf):
        @pl.loop(0, 3)
        def _(j):
            cols = pl.ds(mul(j, 1024), 1024)
            mine = shard[:, pl.ds(pl.multiple_of(c * HALF + j * 1024, 1024), 1024)].astype(F32)
            theirs = other[:, cols].astype(F32)[0:24]
            first = c == 0
            zero = jnp.where(first, mine, theirs)
            one = jnp.where(first, theirs, mine)
            unit = jnp.concatenate([zero, one], axis=0).astype(BF16)
            buf[c, pl.ds(own_row, UNIT), cols] = unit

    own_row = pl.multiple_of(x * PAIR + zl * UNIT, UNIT)
    far_row = pl.multiple_of(x * PAIR + ozl * UNIT, UNIT)

    class Gather:
        def __init__(self, view):
            self.view = view
            self.x, self.core, self.all = {}, {}, []

        def go(self, src, dst, device, landing=None):
            pair = copy(src, dst, device, landing)
            self.all.append(pair)
            return pair[0]

        def unit(self, shift, far, cols=None):
            row = pl.multiple_of(ring(x, shift) * PAIR + (ozl if far else zl) * UNIT, UNIT)
            return self.view(c, pl.ds(row, UNIT), cols)

        def send(self, shift, far, device, land_shift, land_far, cols=None):
            src = self.unit(shift, far, cols)
            return self.go(src, src, device, self.unit(land_shift, land_far, cols))

        def start_z(self):
            self.z = self.send(0, 0, zl_peer, 0, 1)

        def start_x0(self):
            for s in (1, 3):
                self.x[s, 0] = self.send(0, 0, x_peer(s), 4 - s, 0)

        def start_x1(self):
            self.z.wait_recv()
            self.x[3, 1] = self.send(0, 1, x_peer(3), 1, 1)

        def middle(self):
            self.x[1, 0].wait_recv()
            self.x[2, 0] = self.send(3, 0, x_peer(1), 2, 0)
            self.z2 = self.send(3, 0, zl_peer, 3, 1)

        def late(self):
            self.z2.wait_recv()
            self.x[2, 1] = self.send(3, 1, x_peer(1), 2, 1, 0)
            self.x[3, 1].wait_recv()
            self.x[2, 2] = self.send(1, 1, x_peer(3), 2, 1, 1)

        def start_core(self, s):
            if s == 3:
                self.x[3, 0].wait_recv()
            elif s == 2:
                for part in range(3):
                    self.x[2, part].wait_recv()
            rows = pl.ds(mul(ring(x, 4 - s), PAIR), PAIR)
            src = self.view(c, rows)
            self.core[s] = self.go(src, src, core_peer, self.view(oc, rows))

    def quarter(buf, q, rows):
        return buf.at[lax.div(q, 2), rows, pl.ds(pl.multiple_of(lax.rem(q, 2) * QUARTER + c * BLOCK, BLOCK), BLOCK)]

    g_y, g_fwd, x_y = {}, {}, {}

    def start_columns(s):
        gg.core[s].wait_recv()
        row = mul(ring(x, 4 - s), PAIR)
        into = pl.ds(mul(c, BLOCK), BLOCK)
        for r in (1, 3, 2):
            here = gc.at[pl.ds(pl.multiple_of(y * ROWS + row, PAIR), PAIR), into]
            land = gc.at[pl.ds(pl.multiple_of(ring(y, 4 - r) * ROWS + row, PAIR), PAIR), into]
            g_y[r, s] = gg.go(quarter(gb, ring(y, r), pl.ds(row, PAIR)), here, y_peer(r), land)

    def forward_columns(r):
        for s in (0, 1, 3, 2):
            g_y[r, s].wait_recv()
        rows = pl.ds(mul(ring(y, 4 - r), ROWS), ROWS)
        src = gc.at[rows, pl.ds(mul(c, BLOCK), BLOCK)]
        g_fwd[r] = copy(src, src, core_peer, gc.at[rows, pl.ds(mul(oc, BLOCK), BLOCK)])[0]

    def spread_tokens():
        rows = pl.ds(own_row, UNIT)
        for r in (1, 3, 2):
            here, land = xc.at[c, y, rows], xc.at[c, ring(y, 4 - r), rows]
            x_y[r] = gx.go(quarter(xb, ring(y, r), rows), here, y_peer(r), land)
        return local(quarter(xb, y, rows), xc.at[c, y, rows], 2)

    def rows_view(buf):
        def view(half, rows, cols=None):
            return buf.at[half, rows] if cols is None else buf.at[half, rows, pl.ds(cols * QUARTER, QUARTER)]

        return view

    def columns_view(half, rows, cols=None):
        return xc.at[half, :, rows] if cols is None else xc.at[half, :, rows, pl.ds(cols * ROWS, ROWS)]

    gx, gg, gxc = Gather(rows_view(xb)), Gather(rows_view(gb)), Gather(columns_view)
    cg[0].wait_recv()
    assemble(tg, sh.at[1], gb)
    gg.start_z()
    gg.start_x0()
    cx[0].wait_recv()
    assemble(tx, sh.at[0], xb)
    gg.start_x1()
    gg.start_core(0)
    gg.middle()
    gx.start_z()
    gx.start_x0()
    start_columns(0)
    gg.late()
    gg.start_core(1)
    gg.start_core(3)
    gx.start_x1()
    gx.start_core(0)
    start_columns(1)
    start_columns(3)
    gx.middle()
    gx.core[0].wait_recv()
    own_x = spread_tokens()
    gg.start_core(2)
    start_columns(2)
    own_g = local(
        gb.at[lax.div(y, 2), :, pl.ds(mul(lax.rem(y, 2), QUARTER), QUARTER)], gc.at[pl.ds(mul(y, ROWS), ROWS)], 3
    )

    load2.wait()

    @pl.loop(0, 3)
    def _(n):
        cols = pl.ds(mul(n, 256), 256)
        acc2[:, cols] = dot_nt(gb[0], w2[cols, 0:HALF]) + dot_nt(gb[1], w2[cols, HALF:D])

    gx.late()
    own_x.wait()
    for r in (1, 3, 2):
        x_y[r].wait_recv()
    gxc.start_z()
    gxc.start_x0()
    gx.start_core(1)
    gx.start_core(3)
    gx.start_core(2)

    load1.wait()

    @pl.loop(0, 3)
    def _(n):
        cols = pl.ds(mul(n, 256), 256)
        acc[:, cols] = dot(xb[c], w1[pl.ds(mul(c, HALF), HALF), cols])

    for s in (1, 3, 2):
        gx.core[s].wait_recv()

    @pl.loop(0, 3)
    def _(n):
        cols = pl.ds(mul(n, 256), 256)
        acc[:, cols] += dot(xb[oc], w1[pl.ds(mul(oc, HALF), HALF), cols])

    @pl.loop(0, 8)
    def _(i):
        rows = pl.ds(mul(i, UNIT), UNIT)
        u = acc[rows, :]
        t = jnp.tanh(root_coeff * (u + cubic_coeff * u * u * u))
        hb[rows, :] = (0.5 * u * (1.0 + t)).astype(BF16)
        acc[rows, :] = 0.5 * (1.0 + t) + 0.5 * u * (1.0 - t * t) * root_coeff * (
            1.0 + 3.0 * cubic_coeff * u * u
        )

    def transpose_out(rows_ref, into):
        for i in range(3):
            cols = pl.ds(pl.multiple_of(y * ROWS + i * 128, 128), 128)
            into[:, cols] = rows_ref[i * 128 : (i + 1) * 128, :].astype(F32).T.astype(BF16)

    def share(into):
        pairs = {}
        cols = pl.ds(mul(y, ROWS), ROWS)
        for k in range(4):
            for r in (1, 3, 2):
                rows = pl.ds(k * PART, PART)
                src = into.at[rows, cols]
                land = into.at[rows, pl.ds(mul(ring(y, 4 - r), ROWS), ROWS)]
                pairs[r, k] = copy(src, src, y_peer(r), land)[0]
        return pairs

    transpose_out(hb, ht)
    hts = share(ht)
    gxc.start_x1()
    gxc.start_core(0)

    @pl.loop(0, 8)
    def _(i):
        rows = pl.ds(mul(i, UNIT), UNIT)
        pg[rows, :] = (acc2[rows, :] * acc[rows, :]).astype(BF16)

    transpose_out(pg, pt)
    pts = share(pt)
    gxc.middle()
    for r in (1, 3, 2):
        forward_columns(r)

    class Reduce:
        def __init__(self, op, buf, out_ref, product):
            self.op, self.buf, self.out_ref, self.product = op, buf, out_ref, product
            self.core, self.x = {}, {}

        def compute(self, half, j):
            @pl.loop(0, 2)
            def _(n):
                off = j * CHUNK + n * 512
                cols = pl.ds(pl.multiple_of(off, 512), 512)
                part = self.product(pl.multiple_of(half * HALF + off, 512), 512)
                self.buf[half, :, cols] = part.astype(BF16)

        def start_core(self):
            for j in range(3):
                cols = pl.ds(j * CHUNK, CHUNK)
                self.compute(oc, j)
                self.core[j] = copy(self.buf.at[oc, :, cols], rcore.at[:, cols], core_peer)[0]

        def start_x(self):
            for j in range(3):
                cols = pl.ds(j * CHUNK, CHUNK)
                self.compute(c, j)
                self.core[j].wait_recv()

                @pl.loop(0, 8)
                def _(i):
                    rows = pl.ds(mul(i, UNIT), UNIT)
                    both = self.buf[c, rows, cols].astype(F32) + rcore[rows, cols].astype(F32)
                    self.buf[c, rows, cols] = both.astype(BF16)

                for slot, shift, to, part in ((0, 2, 1, 0), (1, 2, 3, 1), (2, 1, 1, 1), (3, 3, 3, 0)):
                    self.send(slot, j, shift, to, part)

        def send(self, slot, j, shift, to, part):
            cols = pl.ds(j * CHUNK, CHUNK)
            src = self.buf.at[c, self.rows(shift, part), cols]
            self.x[slot, j] = copy(src, rx.at[self.op, slot, :, cols], x_peer(to))[0]

        def rows(self, shift, part):
            return pl.ds(pl.multiple_of(ring(x, shift) * PAIR + part * UNIT, UNIT), UNIT)

        def relay(self, j):
            cols = pl.ds(j * CHUNK, CHUNK)
            for slot, to, part in ((0, 1, 0), (1, 3, 1)):
                self.x[slot, j].wait_recv()
                rows = self.rows(to, part)
                both = self.buf[c, rows, cols].astype(F32) + rx[self.op, slot, :, cols].astype(F32)
                self.buf[c, rows, cols] = both.astype(BF16)
                self.send(slot + 4, j, to, to, part)

        def start_z(self):
            for j in range(3):
                for slot in (2, 3, 4, 5):
                    self.x[slot, j].wait_recv()

            @pl.loop(0, 6)
            def _(i):
                cols = pl.ds(mul(i, 512), 512)
                for part, first, second in ((0, 3, 4), (1, 2, 5)):
                    rows = self.rows(0, part)
                    total = self.buf[c, rows, cols].astype(F32)
                    total = total + rx[self.op, first, :, cols].astype(F32)
                    total = total + rx[self.op, second, :, cols].astype(F32)
                    self.buf[c, rows, cols] = total.astype(BF16)

            self.z = copy(self.buf.at[c, pl.ds(far_row, UNIT)], rz.at[self.op], zl_peer)[0]

        def start_last(self):
            self.z.wait_recv()

            @pl.loop(0, 6)
            def _(i):
                cols = pl.ds(mul(i, 512), 512)
                rows = pl.ds(own_row, UNIT)
                total = self.buf[c, rows, cols].astype(F32) + rz[self.op, :, cols].astype(F32)
                self.buf[c, rows, cols] = total.astype(BF16)

            self.last = copy(self.buf.at[c, pl.ds(own_row, UNIT)], rf.at[self.op], core_peer)[0]

        def finish(self):
            self.last.wait_recv()

            def rows_of(value):
                value = value.astype(F32)
                return jnp.where(c == 0, value[0:24], value[24:48]).astype(BF16)

            @pl.loop(0, 3)
            def _(j):
                cols = pl.ds(mul(j, CHUNK), CHUNK)
                mine = self.buf[c, pl.ds(own_row, UNIT), cols]
                theirs = rf[self.op, :, cols]
                self.out_ref[:, pl.ds(pl.multiple_of(c * HALF + j * CHUNK, CHUNK), CHUNK)] = rows_of(mine)
                self.out_ref[:, pl.ds(pl.multiple_of(oc * HALF + j * CHUNK, CHUNK), CHUNK)] = rows_of(theirs)

    red1 = Reduce(0, pb, out_o, lambda at, n: dot(hb[...], w2[:, pl.ds(at, n)]))
    red2 = Reduce(1, gb, tok_o, lambda at, n: dot_nt(pg[...], w1[pl.ds(at, n), :]))
    def out_columns(block, n):
        return gc[:, pl.ds(pl.multiple_of(block * BLOCK + n * 256, 256), 256)]

    def in_columns(block, n):
        return xc[block, :, :, pl.ds(mul(n, 256), 256)].reshape(4 * ROWS, 256)

    def term(rows_ref, columns, rows, block, put):
        @pl.loop(0, 3)
        def _(n):
            put(rows, n, dot(rows_ref[rows, :], columns(block, n)).astype(BF16))

    def whole(rows_ref, columns, put):
        term(rows_ref, columns, slice(0, FH), zh, put)

    def put_w2(base):
        def put(rows, n, value):
            w2[rows, pl.ds(pl.multiple_of(base + n * 256, 256), 256)] = value

        return put

    def put_w1(base):
        def put(rows, n, value):
            w1[base + rows.start : base + rows.stop, pl.ds(mul(n, 256), 256)] = value

        return put

    go_z, gi_z = {}, {}

    def term_out(k):
        for r in (1, 3, 2):
            hts[r, k].wait_recv()
        rows = pl.ds(k * PART, PART)

        def put_xb(_, n, value):
            xb[0, 0:PART, pl.ds(pl.multiple_of(k * BLOCK + n * 256, 256), 256)] = value

        term(ht, out_columns, slice(k * PART, (k + 1) * PART), ozh, put_xb)
        go_z[k] = copy(xb.at[0, 0:PART, k * BLOCK : (k + 1) * BLOCK], zr.at[0, rows], zh_peer)[0]

    def term_in(k):
        for r in (1, 3, 2):
            pts[r, k].wait_recv()
        rows = pl.ds(k * PART, PART)
        term(pt, in_columns, slice(k * PART, (k + 1) * PART), ozh, put_w1(0))
        gi_z[k] = copy(w1.at[rows], zr.at[1, rows], zh_peer)[0]

    red1.start_core()
    for r in (1, 3, 2):
        g_fwd[r].wait_recv()
    own_g.wait()
    finish_sends(gx.all)
    term_out(0)
    gxc.late()
    red1.start_x()
    pl.semaphore_signal(credit, inc=1, device_id=core_peer, device_id_type=MESH)
    term_out(1)
    gxc.start_core(1)
    gxc.start_core(3)
    finish_sends(gg.all)
    pl.semaphore_wait(credit, 1)
    red2.start_core()
    red2.start_x()
    red1.relay(0)
    term_out(2)
    red1.relay(1)
    gxc.start_core(2)
    red1.relay(2)
    term_out(3)
    whole(ht, out_columns, put_w2(BLOCK))
    for s in (0, 1, 3, 2):
        gxc.core[s].wait_recv()
    term_in(0)
    red1.start_z()
    red2.relay(0)
    term_in(1)
    red1.start_last()
    red2.relay(1)
    red2.relay(2)
    term_in(2)
    red1.finish()
    term_in(3)
    red2.start_z()
    whole(pt, in_columns, put_w1(BLOCK))
    red2.start_last()

    for k in range(4):
        go_z[k].wait_recv()

    @pl.loop(0, 8)
    def _(i):
        rows = pl.ds(mul(i, PAIR), PAIR)
        total = w2[rows, BLOCK : 2 * BLOCK].astype(F32) + zr[0, rows, :].astype(F32)
        zr[0, rows, :] = (total * FACTOR).astype(BF16)

    store_o = local(zr.at[0], go_o, 4)
    red2.finish()
    for k in range(4):
        gi_z[k].wait_recv()
        if k % 2:
            for i in range(3):
                lo = (k // 2) * ROWS + i * 128
                total = w1[BLOCK + lo : BLOCK + lo + 128, :].astype(F32) + zr[1, lo : lo + 128, :].astype(F32)
                w1[2 * BLOCK : 3 * BLOCK, lo : lo + 128] = (total * FACTOR).T.astype(BF16)
    store_i = local(w1.at[2 * BLOCK : 3 * BLOCK], gi_o, 5)
    store_o.wait()
    store_i.wait()
    for started in sent:
        if id(started) not in done:
            started.wait_send()


def hand_out(*refs):
    for source, out in zip(refs[:4], refs[4:]):
        out[...] = source[...]


def shards(tokens, out_cotangent, weight_in, weight_out):
    any_space = pl.BlockSpec(memory_space=pl.ANY)
    vmem = pl.BlockSpec(memory_space=pltpu.VMEM)
    out_shape = (
        jax.ShapeDtypeStruct((24, D), BF16),
        jax.ShapeDtypeStruct((24, D), BF16),
        jax.ShapeDtypeStruct((BLOCK, FH), BF16),
        jax.ShapeDtypeStruct((FH, BLOCK), BF16),
    )
    results = pl.pallas_call(
        kernel,
        out_shape=out_shape,
        in_specs=[vmem, vmem, any_space, any_space],
        out_specs=(vmem, vmem, any_space, any_space),
        scratch_shapes=[
            pltpu.VMEM((D, FH), BF16),
            pltpu.VMEM((FH, D), BF16),
            pltpu.VMEM((2, ROWS, HALF), BF16),
            pltpu.VMEM((2, ROWS, HALF), BF16),
            pltpu.VMEM((2, ROWS, HALF), BF16),
            pltpu.VMEM((2, 4, ROWS, BLOCK), BF16),
            pltpu.VMEM((4 * ROWS, QUARTER), BF16),
            pltpu.VMEM((FH, 4 * ROWS), BF16),
            pltpu.VMEM((FH, 4 * ROWS), BF16),
            pltpu.VMEM((2, 32, HALF), BF16),
            pltpu.VMEM((2, 32, HALF), BF16),
            pltpu.VMEM((ROWS, FH), F32),
            pltpu.VMEM((ROWS, FH), F32),
            pltpu.VMEM((ROWS, FH), BF16),
            pltpu.VMEM((ROWS, FH), BF16),
            pltpu.VMEM((ROWS, HALF), BF16),
            pltpu.VMEM((2, 6, UNIT, HALF), BF16),
            pltpu.VMEM((2, UNIT, HALF), BF16),
            pltpu.VMEM((2, UNIT, HALF), BF16),
            pltpu.VMEM((2, BLOCK, BLOCK), BF16),
            pltpu.SemaphoreType.DMA((8,)),
            pltpu.SemaphoreType.DMA((N_COPIES,)),
            pltpu.SemaphoreType.DMA((N_COPIES,)),
            pltpu.SemaphoreType.REGULAR,
        ],
        compiler_params=pltpu.CompilerParams(
            collective_id=0, has_side_effects=True, vmem_limit_bytes=64000 * 1024
        ),
        cost_estimate=pl.CostEstimate(flops=21743271936, bytes_accessed=24000000, transcendentals=294912),
    )(tokens, out_cotangent, weight_in, weight_out)
    blocks = [pl.BlockSpec((24, D // 2), lambda i: (0, i))] * 2 + [pl.BlockSpec((FH // 2, FH), lambda i: (i, 0))] * 2
    return pl.pallas_call(
        hand_out,
        out_shape=out_shape,
        grid=(2,),
        in_specs=blocks,
        out_specs=tuple(blocks),
        compiler_params=pltpu.CompilerParams(vmem_limit_bytes=64000 * 1024),
    )(*results)


def solution(mesh):
    return jax.shard_map(
        shards,
        mesh=mesh,
        in_specs=(P(("dp", "mp"), None), P(("dp", "mp"), None), P(None, "mp"), P("mp", None)),
        out_specs=(P(("dp", "mp"), None), P(("dp", "mp"), None), P("dp", "mp"), P("mp", "dp")),
        check_vma=False,
    )
```

```python
import functools

import jax
import jax.numpy as jnp
from jax import lax
from jax.experimental import pallas as pl
from jax.experimental.pallas import tpu as pltpu
from jax.sharding import PartitionSpec as P

MESH = pl.DeviceIdType.MESH
BF16 = jnp.bfloat16
F32 = jnp.float32
D = 6144
HALF = 3072
QUARTER = 1536
BLOCK = 768
ROWS = 384
UNIT = 48
PAIR = 96
FH = 768
PART = 192
CHUNK = 1024
N_COPIES = 144
FACTOR = 3072.0**-0.5

root_coeff = 0.7978845608028654
cubic_coeff = 0.044715


def mul(value, step):
    return pl.multiple_of(value * step, step)


def dot(left, right):
    return jnp.dot(left, right, preferred_element_type=F32)


def dot_nt(left, right):
    return lax.dot_general(left, right, (((1,), (1,)), ((), ())), preferred_element_type=F32)


def kernel(
    tx, tg, w1_hbm, w2_hbm,
    out_o, tok_o, gi_o, go_o,
    w1, w2, xb, gb, pb, xc, gc, ht, pt, give, sh, acc, acc2, hb, pg, rcore, rx, rz, rf, zr,
    lsem, ssem, rsem, credit,
):
    dp, mp = lax.axis_index("dp"), lax.axis_index("mp")
    y, zh = lax.div(dp, 2), lax.rem(dp, 2)
    zl, x, c = lax.div(mp, 8), lax.rem(lax.div(mp, 2), 4), lax.rem(mp, 2)
    oc, ozl, ozh = 1 - c, 1 - zl, 1 - zh

    def ring(value, shift):
        return lax.rem(value + shift, 4)

    core_peer = (dp, zl * 8 + x * 2 + oc)
    zl_peer = (dp, ozl * 8 + x * 2 + c)
    zh_peer = (y * 2 + ozh, mp)

    def x_peer(shift):
        return (dp, zl * 8 + ring(x, shift) * 2 + c)

    def y_peer(shift):
        return (ring(y, shift) * 2 + zh, mp)

    counter = [0]
    sent, done = [], set()

    def copy(src, dst, device, landing=None):
        at = counter[0]
        counter[0] += 1
        started = pltpu.make_async_remote_copy(
            src_ref=src, dst_ref=dst, send_sem=ssem.at[at], recv_sem=rsem.at[at],
            device_id=device, device_id_type=MESH,
        )
        started.start()
        here = started
        if landing is not None:
            here = pltpu.make_async_remote_copy(
                src_ref=src, dst_ref=landing, send_sem=ssem.at[at], recv_sem=rsem.at[at],
                device_id=device, device_id_type=MESH,
            )
        sent.append(started)
        return here, started

    def finish_sends(pairs):
        for _, started in pairs:
            started.wait_send()
            done.add(id(started))

    barrier = pltpu.get_barrier_semaphore()
    peers = [core_peer, zl_peer, zh_peer] + [x_peer(s) for s in (1, 2, 3)] + [y_peer(s) for s in (1, 2, 3)]
    for peer in peers:
        pl.semaphore_signal(barrier, inc=1, device_id=peer, device_id_type=MESH)
    pl.semaphore_wait(barrier, len(peers))

    def local(src, dst, at):
        started = pltpu.make_async_copy(src, dst, lsem.at[at])
        started.start()
        return started

    def hand_over(shard, at):
        @pl.loop(0, 3)
        def _(j):
            theirs = shard[:, pl.ds(pl.multiple_of(oc * HALF + j * 1024, 1024), 1024)].astype(F32)
            padded = jnp.concatenate([theirs, jnp.zeros((8, 1024), F32)], axis=0)
            give[at, :, pl.ds(mul(j, 1024), 1024)] = padded.astype(BF16)

        return copy(give.at[at], sh.at[at], core_peer)

    cg = hand_over(tg, 1)
    cx = hand_over(tx, 0)
    load2 = local(w2_hbm, w2, 1)
    load1 = local(w1_hbm, w1, 0)

    def assemble(shard, other, buf):
        @pl.loop(0, 3)
        def _(j):
            cols = pl.ds(mul(j, 1024), 1024)
            mine = shard[:, pl.ds(pl.multiple_of(c * HALF + j * 1024, 1024), 1024)].astype(F32)
            theirs = other[:, cols].astype(F32)[0:24]
            first = c == 0
            zero = jnp.where(first, mine, theirs)
            one = jnp.where(first, theirs, mine)
            unit = jnp.concatenate([zero, one], axis=0).astype(BF16)
            buf[c, pl.ds(own_row, UNIT), cols] = unit

    own_row = pl.multiple_of(x * PAIR + zl * UNIT, UNIT)
    far_row = pl.multiple_of(x * PAIR + ozl * UNIT, UNIT)

    class Gather:
        def __init__(self, view):
            self.view = view
            self.x, self.core, self.all = {}, {}, []

        def go(self, src, dst, device, landing=None):
            pair = copy(src, dst, device, landing)
            self.all.append(pair)
            return pair[0]

        def unit(self, shift, far, cols=None):
            row = pl.multiple_of(ring(x, shift) * PAIR + (ozl if far else zl) * UNIT, UNIT)
            return self.view(c, pl.ds(row, UNIT), cols)

        def send(self, shift, far, device, land_shift, land_far, cols=None):
            src = self.unit(shift, far, cols)
            return self.go(src, src, device, self.unit(land_shift, land_far, cols))

        def start_z(self):
            self.z = self.send(0, 0, zl_peer, 0, 1)

        def start_x0(self):
            for s in (1, 3):
                self.x[s, 0] = self.send(0, 0, x_peer(s), 4 - s, 0)

        def start_x1(self):
            self.z.wait_recv()
            self.x[3, 1] = self.send(0, 1, x_peer(3), 1, 1)

        def middle(self):
            self.x[1, 0].wait_recv()
            self.x[2, 0] = self.send(3, 0, x_peer(1), 2, 0)
            self.z2 = self.send(3, 0, zl_peer, 3, 1)

        def late(self):
            self.z2.wait_recv()
            self.x[2, 1] = self.send(3, 1, x_peer(1), 2, 1, 0)
            self.x[3, 1].wait_recv()
            self.x[2, 2] = self.send(1, 1, x_peer(3), 2, 1, 1)

        def start_core(self, s):
            if s == 3:
                self.x[3, 0].wait_recv()
            elif s == 2:
                for part in range(3):
                    self.x[2, part].wait_recv()
            rows = pl.ds(mul(ring(x, 4 - s), PAIR), PAIR)
            src = self.view(c, rows)
            self.core[s] = self.go(src, src, core_peer, self.view(oc, rows))

    def quarter(buf, q, rows):
        return buf.at[lax.div(q, 2), rows, pl.ds(pl.multiple_of(lax.rem(q, 2) * QUARTER + c * BLOCK, BLOCK), BLOCK)]

    g_y, g_fwd, x_y = {}, {}, {}

    def start_columns(s):
        gg.core[s].wait_recv()
        row = mul(ring(x, 4 - s), PAIR)
        into = pl.ds(mul(c, BLOCK), BLOCK)
        for r in (1, 3, 2):
            here = gc.at[pl.ds(pl.multiple_of(y * ROWS + row, PAIR), PAIR), into]
            land = gc.at[pl.ds(pl.multiple_of(ring(y, 4 - r) * ROWS + row, PAIR), PAIR), into]
            g_y[r, s] = gg.go(quarter(gb, ring(y, r), pl.ds(row, PAIR)), here, y_peer(r), land)

    def forward_columns(r):
        for s in (0, 1, 3, 2):
            g_y[r, s].wait_recv()
        rows = pl.ds(mul(ring(y, 4 - r), ROWS), ROWS)
        src = gc.at[rows, pl.ds(mul(c, BLOCK), BLOCK)]
        g_fwd[r] = copy(src, src, core_peer, gc.at[rows, pl.ds(mul(oc, BLOCK), BLOCK)])[0]

    def spread_tokens():
        rows = pl.ds(own_row, UNIT)
        for r in (1, 3, 2):
            here, land = xc.at[c, y, rows], xc.at[c, ring(y, 4 - r), rows]
            x_y[r] = gx.go(quarter(xb, ring(y, r), rows), here, y_peer(r), land)
        return local(quarter(xb, y, rows), xc.at[c, y, rows], 2)

    def rows_view(buf):
        def view(half, rows, cols=None):
            return buf.at[half, rows] if cols is None else buf.at[half, rows, pl.ds(cols * QUARTER, QUARTER)]

        return view

    def columns_view(half, rows, cols=None):
        return xc.at[half, :, rows] if cols is None else xc.at[half, :, rows, pl.ds(cols * ROWS, ROWS)]

    gx, gg, gxc = Gather(rows_view(xb)), Gather(rows_view(gb)), Gather(columns_view)
    cg[0].wait_recv()
    assemble(tg, sh.at[1], gb)
    gg.start_z()
    gg.start_x0()
    cx[0].wait_recv()
    assemble(tx, sh.at[0], xb)
    gg.start_x1()
    gg.start_core(0)
    gg.middle()
    gx.start_z()
    gx.start_x0()
    start_columns(0)
    gg.late()
    gg.start_core(1)
    gg.start_core(3)
    gx.start_x1()
    gx.start_core(0)
    start_columns(1)
    start_columns(3)
    gx.middle()
    gx.core[0].wait_recv()
    own_x = spread_tokens()
    gg.start_core(2)
    start_columns(2)
    own_g = local(
        gb.at[lax.div(y, 2), :, pl.ds(mul(lax.rem(y, 2), QUARTER), QUARTER)], gc.at[pl.ds(mul(y, ROWS), ROWS)], 3
    )

    load2.wait()

    @pl.loop(0, 3)
    def _(n):
        cols = pl.ds(mul(n, 256), 256)
        acc2[:, cols] = dot_nt(gb[0], w2[cols, 0:HALF]) + dot_nt(gb[1], w2[cols, HALF:D])

    gx.late()
    own_x.wait()
    for r in (1, 3, 2):
        x_y[r].wait_recv()
    gxc.start_z()
    gxc.start_x0()
    gx.start_core(1)
    gx.start_core(3)
    gx.start_core(2)

    load1.wait()

    @pl.loop(0, 3)
    def _(n):
        cols = pl.ds(mul(n, 256), 256)
        acc[:, cols] = dot(xb[c], w1[pl.ds(mul(c, HALF), HALF), cols])

    for s in (1, 3, 2):
        gx.core[s].wait_recv()

    @pl.loop(0, 3)
    def _(n):
        cols = pl.ds(mul(n, 256), 256)
        acc[:, cols] += dot(xb[oc], w1[pl.ds(mul(oc, HALF), HALF), cols])

    @pl.loop(0, 8)
    def _(i):
        rows = pl.ds(mul(i, UNIT), UNIT)
        u = acc[rows, :]
        t = jnp.tanh(root_coeff * (u + cubic_coeff * u * u * u))
        hb[rows, :] = (0.5 * u * (1.0 + t)).astype(BF16)
        acc[rows, :] = 0.5 * (1.0 + t) + 0.5 * u * (1.0 - t * t) * root_coeff * (
            1.0 + 3.0 * cubic_coeff * u * u
        )

    def transpose_out(rows_ref, into):
        for i in range(3):
            cols = pl.ds(pl.multiple_of(y * ROWS + i * 128, 128), 128)
            into[:, cols] = rows_ref[i * 128 : (i + 1) * 128, :].astype(F32).T.astype(BF16)

    def share(into):
        pairs = {}
        cols = pl.ds(mul(y, ROWS), ROWS)
        for k in range(4):
            for r in (1, 3, 2):
                rows = pl.ds(k * PART, PART)
                src = into.at[rows, cols]
                land = into.at[rows, pl.ds(mul(ring(y, 4 - r), ROWS), ROWS)]
                pairs[r, k] = copy(src, src, y_peer(r), land)[0]
        return pairs

    transpose_out(hb, ht)
    hts = share(ht)
    gxc.start_x1()
    gxc.start_core(0)

    @pl.loop(0, 8)
    def _(i):
        rows = pl.ds(mul(i, UNIT), UNIT)
        pg[rows, :] = (acc2[rows, :] * acc[rows, :]).astype(BF16)

    transpose_out(pg, pt)
    pts = share(pt)
    gxc.middle()
    for r in (1, 3, 2):
        forward_columns(r)

    class Reduce:
        def __init__(self, op, buf, out_ref, product):
            self.op, self.buf, self.out_ref, self.product = op, buf, out_ref, product
            self.core, self.x = {}, {}

        def compute(self, half, j):
            @pl.loop(0, 2)
            def _(n):
                off = j * CHUNK + n * 512
                cols = pl.ds(pl.multiple_of(off, 512), 512)
                part = self.product(pl.multiple_of(half * HALF + off, 512), 512)
                self.buf[half, :, cols] = part.astype(BF16)

        def start_core(self):
            for j in range(3):
                cols = pl.ds(j * CHUNK, CHUNK)
                self.compute(oc, j)
                self.core[j] = copy(self.buf.at[oc, :, cols], rcore.at[:, cols], core_peer)[0]

        def start_x(self):
            for j in range(3):
                cols = pl.ds(j * CHUNK, CHUNK)
                self.compute(c, j)
                self.core[j].wait_recv()

                @pl.loop(0, 8)
                def _(i):
                    rows = pl.ds(mul(i, UNIT), UNIT)
                    both = self.buf[c, rows, cols].astype(F32) + rcore[rows, cols].astype(F32)
                    self.buf[c, rows, cols] = both.astype(BF16)

                for slot, shift, to, part in ((0, 2, 1, 0), (1, 2, 3, 1), (2, 1, 1, 1), (3, 3, 3, 0)):
                    self.send(slot, j, shift, to, part)

        def send(self, slot, j, shift, to, part):
            cols = pl.ds(j * CHUNK, CHUNK)
            src = self.buf.at[c, self.rows(shift, part), cols]
            self.x[slot, j] = copy(src, rx.at[self.op, slot, :, cols], x_peer(to))[0]

        def rows(self, shift, part):
            return pl.ds(pl.multiple_of(ring(x, shift) * PAIR + part * UNIT, UNIT), UNIT)

        def relay(self, j):
            cols = pl.ds(j * CHUNK, CHUNK)
            for slot, to, part in ((0, 1, 0), (1, 3, 1)):
                self.x[slot, j].wait_recv()
                rows = self.rows(to, part)
                both = self.buf[c, rows, cols].astype(F32) + rx[self.op, slot, :, cols].astype(F32)
                self.buf[c, rows, cols] = both.astype(BF16)
                self.send(slot + 4, j, to, to, part)

        def start_z(self):
            for j in range(3):
                for slot in (2, 3, 4, 5):
                    self.x[slot, j].wait_recv()

            @pl.loop(0, 6)
            def _(i):
                cols = pl.ds(mul(i, 512), 512)
                for part, first, second in ((0, 3, 4), (1, 2, 5)):
                    rows = self.rows(0, part)
                    total = self.buf[c, rows, cols].astype(F32)
                    total = total + rx[self.op, first, :, cols].astype(F32)
                    total = total + rx[self.op, second, :, cols].astype(F32)
                    self.buf[c, rows, cols] = total.astype(BF16)

            self.z = copy(self.buf.at[c, pl.ds(far_row, UNIT)], rz.at[self.op], zl_peer)[0]

        def start_last(self):
            self.z.wait_recv()

            @pl.loop(0, 6)
            def _(i):
                cols = pl.ds(mul(i, 512), 512)
                rows = pl.ds(own_row, UNIT)
                total = self.buf[c, rows, cols].astype(F32) + rz[self.op, :, cols].astype(F32)
                self.buf[c, rows, cols] = total.astype(BF16)

            self.last = copy(self.buf.at[c, pl.ds(own_row, UNIT)], rf.at[self.op], core_peer)[0]

        def finish(self):
            self.last.wait_recv()

            def rows_of(value):
                value = value.astype(F32)
                return jnp.where(c == 0, value[0:24], value[24:48]).astype(BF16)

            @pl.loop(0, 3)
            def _(j):
                cols = pl.ds(mul(j, CHUNK), CHUNK)
                mine = self.buf[c, pl.ds(own_row, UNIT), cols]
                theirs = rf[self.op, :, cols]
                self.out_ref[:, pl.ds(pl.multiple_of(c * HALF + j * CHUNK, CHUNK), CHUNK)] = rows_of(mine)
                self.out_ref[:, pl.ds(pl.multiple_of(oc * HALF + j * CHUNK, CHUNK), CHUNK)] = rows_of(theirs)

    red1 = Reduce(0, pb, out_o, lambda at, n: dot(hb[...], w2[:, pl.ds(at, n)]))
    red2 = Reduce(1, gb, tok_o, lambda at, n: dot_nt(pg[...], w1[pl.ds(at, n), :]))
    def out_columns(block, n):
        return gc[:, pl.ds(pl.multiple_of(block * BLOCK + n * 256, 256), 256)]

    def in_columns(block, n):
        return xc[block, :, :, pl.ds(mul(n, 256), 256)].reshape(4 * ROWS, 256)

    def term(rows_ref, columns, rows, block, put):
        @pl.loop(0, 3)
        def _(n):
            put(rows, n, dot(rows_ref[rows, :], columns(block, n)).astype(BF16))

    def whole(rows_ref, columns, put):
        term(rows_ref, columns, slice(0, FH), zh, put)

    def put_w2(base):
        def put(rows, n, value):
            w2[rows, pl.ds(pl.multiple_of(base + n * 256, 256), 256)] = value

        return put

    def put_w1(base):
        def put(rows, n, value):
            w1[base + rows.start : base + rows.stop, pl.ds(mul(n, 256), 256)] = value

        return put

    go_z, gi_z = {}, {}

    def term_out(k):
        for r in (1, 3, 2):
            hts[r, k].wait_recv()
        rows = pl.ds(k * PART, PART)

        def put_xb(_, n, value):
            xb[0, 0:PART, pl.ds(pl.multiple_of(k * BLOCK + n * 256, 256), 256)] = value

        term(ht, out_columns, slice(k * PART, (k + 1) * PART), ozh, put_xb)
        go_z[k] = copy(xb.at[0, 0:PART, k * BLOCK : (k + 1) * BLOCK], zr.at[0, rows], zh_peer)[0]

    def term_in(k):
        for r in (1, 3, 2):
            pts[r, k].wait_recv()
        rows = pl.ds(k * PART, PART)
        term(pt, in_columns, slice(k * PART, (k + 1) * PART), ozh, put_w1(0))
        gi_z[k] = copy(w1.at[rows], zr.at[1, rows], zh_peer)[0]

    red1.start_core()
    for r in (1, 3, 2):
        g_fwd[r].wait_recv()
    own_g.wait()
    finish_sends(gx.all)
    term_out(0)
    gxc.late()
    red1.start_x()
    pl.semaphore_signal(credit, inc=1, device_id=core_peer, device_id_type=MESH)
    term_out(1)
    gxc.start_core(1)
    gxc.start_core(3)
    finish_sends(gg.all)
    pl.semaphore_wait(credit, 1)
    red2.start_core()
    red2.start_x()
    red1.relay(0)
    term_out(2)
    red1.relay(1)
    gxc.start_core(2)
    red1.relay(2)
    term_out(3)
    whole(ht, out_columns, put_w2(BLOCK))
    for s in (0, 1, 3, 2):
        gxc.core[s].wait_recv()
    term_in(0)
    red1.start_z()
    red2.relay(0)
    term_in(1)
    red1.start_last()
    red2.relay(1)
    red2.relay(2)
    term_in(2)
    red1.finish()
    term_in(3)
    red2.start_z()
    whole(pt, in_columns, put_w1(BLOCK))
    red2.start_last()

    for k in range(4):
        go_z[k].wait_recv()

    @pl.loop(0, 8)
    def _(i):
        rows = pl.ds(mul(i, PAIR), PAIR)
        total = w2[rows, BLOCK : 2 * BLOCK].astype(F32) + zr[0, rows, :].astype(F32)
        zr[0, rows, :] = (total * FACTOR).astype(BF16)

    store_o = local(zr.at[0], go_o, 4)
    red2.finish()
    for k in range(4):
        gi_z[k].wait_recv()
        if k % 2:
            for i in range(3):
                lo = (k // 2) * ROWS + i * 128
                total = w1[BLOCK + lo : BLOCK + lo + 128, :].astype(F32) + zr[1, lo : lo + 128, :].astype(F32)
                w1[2 * BLOCK : 3 * BLOCK, lo : lo + 128] = (total * FACTOR).T.astype(BF16)
    store_i = local(w1.at[2 * BLOCK : 3 * BLOCK], gi_o, 5)
    store_o.wait()
    store_i.wait()
    for started in sent:
        if id(started) not in done:
            started.wait_send()


def hand_out(*refs):
    for source, out in zip(refs[:4], refs[4:]):
        out[...] = source[...]


def shards(tokens, out_cotangent, weight_in, weight_out):
    any_space = pl.BlockSpec(memory_space=pl.ANY)
    vmem = pl.BlockSpec(memory_space=pltpu.VMEM)
    out_shape = (
        jax.ShapeDtypeStruct((24, D), BF16),
        jax.ShapeDtypeStruct((24, D), BF16),
        jax.ShapeDtypeStruct((BLOCK, FH), BF16),
        jax.ShapeDtypeStruct((FH, BLOCK), BF16),
    )
    results = pl.pallas_call(
        kernel,
        out_shape=out_shape,
        in_specs=[vmem, vmem, any_space, any_space],
        out_specs=(vmem, vmem, any_space, any_space),
        scratch_shapes=[
            pltpu.VMEM((D, FH), BF16),
            pltpu.VMEM((FH, D), BF16),
            pltpu.VMEM((2, ROWS, HALF), BF16),
            pltpu.VMEM((2, ROWS, HALF), BF16),
            pltpu.VMEM((2, ROWS, HALF), BF16),
            pltpu.VMEM((2, 4, ROWS, BLOCK), BF16),
            pltpu.VMEM((4 * ROWS, QUARTER), BF16),
            pltpu.VMEM((FH, 4 * ROWS), BF16),
            pltpu.VMEM((FH, 4 * ROWS), BF16),
            pltpu.VMEM((2, 32, HALF), BF16),
            pltpu.VMEM((2, 32, HALF), BF16),
            pltpu.VMEM((ROWS, FH), F32),
            pltpu.VMEM((ROWS, FH), F32),
            pltpu.VMEM((ROWS, FH), BF16),
            pltpu.VMEM((ROWS, FH), BF16),
            pltpu.VMEM((ROWS, HALF), BF16),
            pltpu.VMEM((2, 6, UNIT, HALF), BF16),
            pltpu.VMEM((2, UNIT, HALF), BF16),
            pltpu.VMEM((2, UNIT, HALF), BF16),
            pltpu.VMEM((2, BLOCK, BLOCK), BF16),
            pltpu.SemaphoreType.DMA((8,)),
            pltpu.SemaphoreType.DMA((N_COPIES,)),
            pltpu.SemaphoreType.DMA((N_COPIES,)),
            pltpu.SemaphoreType.REGULAR,
        ],
        compiler_params=pltpu.CompilerParams(
            collective_id=0, has_side_effects=True, vmem_limit_bytes=64000 * 1024
        ),
        cost_estimate=pl.CostEstimate(flops=21743271936, bytes_accessed=24000000, transcendentals=294912),
    )(tokens, out_cotangent, weight_in, weight_out)
    blocks = [pl.BlockSpec((24, D), lambda i: (0, i))] * 2 + [pl.BlockSpec((FH, FH), lambda i: (i, 0))] * 2
    return pl.pallas_call(
        hand_out,
        out_shape=out_shape,
        grid=(1,),
        in_specs=blocks,
        out_specs=tuple(blocks),
        compiler_params=pltpu.CompilerParams(vmem_limit_bytes=64000 * 1024),
    )(*results)


def solution(mesh):
    return jax.shard_map(
        shards,
        mesh=mesh,
        in_specs=(P(("dp", "mp"), None), P(("dp", "mp"), None), P(None, "mp"), P("mp", None)),
        out_specs=(P(("dp", "mp"), None), P(("dp", "mp"), None), P("dp", "mp"), P("mp", "dp")),
        check_vma=False,
    )
```
